32 devices in a mesh: space: 8 (over y, x, core), bins: 4 (over z).
Axes of the slice: x: 2, y: 2, z: 4, core: 2. Of those that a mesh axis runs over, the one named last changes fastest.
Arguments:
- population: float32 [256, 24, 32, 128], P('bins', 'space'), may hold values from 0 to 2
- velocity: bfloat16 [3, 24, 32, 128], P(None, 'space'), may hold values from -1 to 1
- supersat: float32 [24, 32, 128], P('space', 'bins'), may hold values from 0.2 to 1.5
- kernel: float32 [256], replicated, may hold values from 0.0005 to 0.004
Outputs:
- new_population: float32 [256, 24, 32, 128], P(None, 'space', 'bins')
- depletion: float32 [24, 32, 128], P('space')
The draws below stay inside these ranges and needn't reach their ends.
All inputs are finite; a program needn't handle non-finite values.
Results may differ from the reference program's by a relative error of at most 0.0006.
Values may be sent and summed in bfloat16 or wider, within the bound.
No kernel may reach another device: no remote copies, remote signals or barrier semaphores. Data moves between devices by JAX's collectives and lax.ppermute only.
A program may use at most 64 MiB of HBM per device.

```python
import math
import jax
import jax.numpy as jnp
from jax import lax

BINS = 256
NY = 32
NZ = 128
STEPS = 3
KSTEPS = 8
NX = 24


def block_levels(key, dims, split, low, top_value):
    loudness, own = 1.0, jax.random.fold_in(key, 6)
    for dim, shards_of in split:
        heights = jnp.exp(jax.random.uniform(jax.random.fold_in(own, dim), (shards_of,), jnp.float32, low / len(split), top_value / len(split)))
        loudness = loudness * jnp.repeat(heights, dims[dim] // shards_of).reshape([-1 if axis == dim else 1 for axis in range(len(dims))])
    return loudness


def setup_inputs(seed: int = 0) -> dict:
    arg_keys = jax.random.split(jax.random.key(seed), 5)
    population = jnp.clip(2.0 * jax.random.uniform(arg_keys[0], (BINS, NX, NY, NZ), jnp.float32) ** block_levels(arg_keys[0], (BINS, NX, NY, NZ), ((0, 4), (1, 8)), -0.2, 0.2), 0.0, 2.0)
    velocity = jnp.clip(jax.random.uniform(arg_keys[1], (3, NX, NY, NZ), jnp.float32, -1.0, 1.0) * block_levels(arg_keys[1], (3, NX, NY, NZ), ((1, 8),), -0.4, 0.0), -1.0, 1.0).astype(jnp.bfloat16)
    supersat = jnp.clip(0.2 + 1.3 * jax.random.uniform(arg_keys[2], (NX, NY, NZ), jnp.float32) ** block_levels(arg_keys[2], (NX, NY, NZ), ((0, 8), (1, 4)), -0.2, 0.2), 0.2, 1.5)
    kernel = jnp.clip(jnp.exp(jax.random.uniform(arg_keys[3], (BINS,), jnp.float32, math.log(0.0005), math.log(0.004))), 0.0005, 0.004)
    return {"population": population, "velocity": velocity, "supersat": supersat, "kernel": kernel}


COURANT = 0.3
GROW = 0.4
BETA = 0.5


def advance(density, vel_padded):
    vel = vel_padded.astype(jnp.float32)
    span_x = density.shape[1] - 2
    span_y = density.shape[2] - 2
    vel_x = vel[0, 1:span_x + 2, 1:span_y + 1]
    flux_x = jnp.maximum(vel_x, 0.0) * density[:, 0:span_x + 1, 1:span_y + 1] + jnp.minimum(vel_x, 0.0) * density[:, 1:span_x + 2, 1:span_y + 1]
    outflow = flux_x[:, 1:] - flux_x[:, :-1]
    vel_y = vel[1, 1:span_x + 1, 1:span_y + 2]
    flux_y = jnp.maximum(vel_y, 0.0) * density[:, 1:span_x + 1, 0:span_y + 1] + jnp.minimum(vel_y, 0.0) * density[:, 1:span_x + 1, 1:span_y + 2]
    outflow = outflow + flux_y[:, :, 1:] - flux_y[:, :, :-1]
    centre = density[:, 1:span_x + 1, 1:span_y + 1]
    count_z = centre.shape[3]
    padded_z = jnp.pad(centre, ((0, 0), (0, 0), (0, 0), (1, 1)))
    vel_z = jnp.pad(vel[2, 1:span_x + 1, 1:span_y + 1], ((0, 0), (0, 0), (0, 1)))
    flux_z = jnp.maximum(vel_z, 0.0) * padded_z[..., 0:count_z + 1] + jnp.minimum(vel_z, 0.0) * padded_z[..., 1:count_z + 2]
    outflow = outflow + flux_z[..., 1:] - flux_z[..., :-1]
    return centre - COURANT * outflow


def kinetics(columns, supersat, kernel):
    bin_count = kernel.shape[0]
    row_index = jnp.arange(bin_count, dtype=jnp.int32)[:, None]
    col_index = jnp.arange(bin_count, dtype=jnp.int32)[None, :]
    offsets = row_index - col_index
    toeplitz = jnp.where(offsets >= 0, kernel[jnp.clip(offsets, 0, bin_count - 1)], 0.0).astype(jnp.bfloat16)
    colsum = jnp.cumsum(kernel)[::-1][:, None]
    masses = ((jnp.arange(bin_count, dtype=jnp.float32) + 1.0) / bin_count) ** 3
    initial = columns
    for substep in range(KSTEPS):
        product = jnp.dot(toeplitz, columns.astype(jnp.bfloat16), preferred_element_type=jnp.float32)
        lower_bins = jnp.pad(columns[:-1], ((1, 0), (0, 0)))
        columns = columns + GROW * supersat * (lower_bins - columns) + BETA * supersat * (product - colsum * columns)
    depletion = jnp.sum(masses[:, None] * (columns - initial), axis=0)
    return columns, depletion


def reference(population, velocity, supersat, kernel):
    vel_padded = jnp.pad(velocity, ((0, 0), (1, 1), (1, 1), (0, 0)))

    def sweeps(bin_block):
        for sweep in range(STEPS):
            bin_block = advance(jnp.pad(bin_block, ((0, 0), (1, 1), (1, 1), (0, 0))), vel_padded)
        return bin_block

    grouped = population.reshape(BINS // 16, 16, NX, NY, NZ)
    moved = lax.map(sweeps, grouped).reshape(BINS, NX, NY, NZ)
    slabs = jnp.moveaxis(moved, 1, 0).reshape(NX, BINS, NY * NZ)

    def kinetic_slab(paired):
        return kinetics(paired[0], paired[1], kernel)

    updated, depletion = lax.map(kinetic_slab, (slabs, supersat.reshape(NX, NY * NZ)))
    new_population = jnp.moveaxis(updated.reshape(NX, BINS, NY, NZ), 0, 1)
    return new_population, depletion.reshape(NX, NY, NZ)
```

```python
import jax
import jax.numpy as jnp
from jax import lax
from jax.sharding import PartitionSpec as P

STEPS = 3
KSTEPS = 8


COURANT = 0.3
GROW = 0.4
BETA = 0.5


def passed_along(array, axis, by):
    count = lax.axis_size(axis)
    pairs = [(i, i + by) for i in range(count) if 0 <= i + by < count]
    return lax.ppermute(array, axis, pairs)


def padded(array, sides, width):
    for axis, dim in sides:
        count, length = (lax.axis_size(axis), array.shape[dim])
        up = [(i, (i + 1) % count) for i in range(count - 1)]
        down = [(j, i) for i, j in up]
        last = lax.slice_in_dim(array, length - width, length, axis=dim)
        initial = lax.slice_in_dim(array, 0, width, axis=dim)
        before = lax.ppermute(last, axis, up)
        after = lax.ppermute(initial, axis, down)
        array = jnp.concatenate([before, array, after], axis=dim)
    return array


def advance(density, vel_padded):
    vel = vel_padded.astype(jnp.float32)
    span_x = density.shape[1] - 2
    span_y = density.shape[2] - 2
    vel_x = vel[0, 1 : span_x + 2, 1 : span_y + 1]
    flux_x = (
        jnp.maximum(vel_x, 0.0) * density[:, 0 : span_x + 1, 1 : span_y + 1]
        + jnp.minimum(vel_x, 0.0) * density[:, 1 : span_x + 2, 1 : span_y + 1]
    )
    outflow = flux_x[:, 1:] - flux_x[:, :-1]
    vel_y = vel[1, 1 : span_x + 1, 1 : span_y + 2]
    flux_y = (
        jnp.maximum(vel_y, 0.0) * density[:, 1 : span_x + 1, 0 : span_y + 1]
        + jnp.minimum(vel_y, 0.0) * density[:, 1 : span_x + 1, 1 : span_y + 2]
    )
    outflow = outflow + flux_y[:, :, 1:] - flux_y[:, :, :-1]
    centre = density[:, 1 : span_x + 1, 1 : span_y + 1]
    count_z = centre.shape[3]
    padded_z = jnp.pad(centre, ((0, 0), (0, 0), (0, 0), (1, 1)))
    vel_z = jnp.pad(vel[2, 1 : span_x + 1, 1 : span_y + 1], ((0, 0), (0, 0), (0, 1)))
    flux_z = (
        jnp.maximum(vel_z, 0.0) * padded_z[..., 0 : count_z + 1]
        + jnp.minimum(vel_z, 0.0) * padded_z[..., 1 : count_z + 2]
    )
    outflow = outflow + flux_z[..., 1:] - flux_z[..., :-1]
    return centre - COURANT * outflow


def kinetics(columns, supersat, kernel):
    bin_count = kernel.shape[0]
    wide = jnp.concatenate([kernel, jnp.zeros_like(kernel)]).astype(jnp.bfloat16)
    span = 2 * bin_count
    rows = jnp.tile(wide, bin_count)[: bin_count * (span - 1)].reshape(bin_count, span - 1)
    toeplitz = rows[:, :bin_count].T
    colsum = jnp.cumsum(kernel)[::-1][:, None]
    masses = ((jnp.arange(bin_count, dtype=jnp.float32) + 1.0) / bin_count) ** 3
    initial = columns
    for substep in range(KSTEPS):
        product = jnp.dot(
            toeplitz, columns.astype(jnp.bfloat16), preferred_element_type=jnp.float32
        )
        lower_bins = jnp.pad(columns[:-1], ((1, 0), (0, 0)))
        columns = (
            columns
            + GROW * supersat * (lower_bins - columns)
            + BETA * supersat * (product - colsum * columns)
        )
    depletion = jnp.sum(masses[:, None] * (columns - initial), axis=0)
    return (columns, depletion)


def pad_second(values):
    return jnp.pad(values, ((0, 0), (0, 0), (1, 1), (0, 0)))


def body(population, velocity, supersat, kernel):
    slab_steps = STEPS
    density = population
    above = passed_along(velocity[:, 0:1], "space", -1)
    vel_rows = jnp.concatenate([jnp.zeros_like(above), velocity, above], axis=1)
    vel_near = pad_second(vel_rows)
    for sweep in range(slab_steps):
        rimmed = padded(density, (("space", 1),), 1)
        density = advance(pad_second(rimmed), vel_near)
    batches = lax.all_to_all(density, "bins", split_axis=2, concat_axis=0, tiled=True)
    bin_count = batches.shape[0]
    updated, depletion = kinetics(batches.reshape(bin_count, -1), supersat.reshape(-1), kernel)
    new_population = updated.reshape(batches.shape)
    depletion = lax.all_gather(depletion.reshape(supersat.shape), "bins", axis=1, tiled=True)
    return (new_population, depletion)


def solution(mesh):
    in_specs = (
        P("bins", "space", None, None),
        P(None, "space", None, None),
        P("space", "bins", None),
        P(),
    )
    out_specs = (P(None, "space", "bins", None), P("space", None, None))
    return jax.shard_map(body, mesh=mesh, in_specs=in_specs, out_specs=out_specs, check_vma=False)
```

```python
import functools

import jax
import jax.numpy as jnp
from jax import lax
from jax.experimental import pallas as pl
from jax.experimental.pallas import tpu as pltpu
from jax.sharding import PartitionSpec as P

STEPS = 3
KSTEPS = 8

COURANT = 0.3
GROW = 0.4
BETA = 0.5

POWER = 9
SCALE = 256.0
GROUP = 16
VMEM_LIMIT = 48 * 1024 * 1024


def encode(scaled):
    square = scaled * scaled
    fourth = square * square
    return (fourth * fourth * scaled).astype(jnp.bfloat16)


def decode(code):
    wide = code.astype(jnp.float32)
    size = jnp.exp(jnp.log(jnp.abs(wide)) * (1.0 / POWER))
    return jnp.where(wide < 0.0, -size, size)


def params():
    return pltpu.CompilerParams(vmem_limit_bytes=VMEM_LIMIT)


def vmem_spec():
    return pl.BlockSpec(memory_space=pltpu.VMEM)


def cells_first(block_ref, x, y, bins, span_x, span_y):
    rows = block_ref.reshape(bins * span_x * span_y, block_ref.shape[3])
    return rows[pl.ds(x * span_y + y, bins, stride=span_x * span_y), :]


def code_kernel(pop_ref, code_ref):
    bins, span_x, span_y, _ = pop_ref.shape
    for x in range(span_x):

        def row(y, carry, x=x):
            code_ref[x, y] = encode(cells_first(pop_ref, x, y, bins, span_x, span_y) * SCALE)
            return carry

        lax.fori_loop(0, span_y, row, 0, unroll=4)


def coded_slab(population, index):
    _, span_x, span_y, span_z = population.shape
    return pl.pallas_call(
        code_kernel,
        grid=(1,),
        in_specs=[pl.BlockSpec((GROUP, span_x, span_y, span_z), lambda i: (index, 0, 0, 0))],
        out_specs=pl.BlockSpec((span_x, span_y, GROUP, span_z), lambda i: (0, 0, 0, 0)),
        out_shape=jax.ShapeDtypeStruct((span_x, span_y, GROUP, span_z), jnp.bfloat16),
        compiler_params=params(),
        name="code_slab",
    )(population)


def stencil(src_ref, coef_ref, x, y, shift):
    span_z = src_ref.shape[3]
    centre = src_ref[x + 1, y + 1]
    weight = lambda k: coef_ref[x + shift, y, pl.ds(k, 1), :]
    total = weight(0) * centre
    total += weight(1) * src_ref[x, y + 1]
    total += weight(2) * src_ref[x + 2, y + 1]
    total += weight(3) * src_ref[x + 1, y]
    total += weight(4) * src_ref[x + 1, y + 2]
    total += weight(5) * pltpu.roll(centre, 1, 1)
    total += weight(6) * pltpu.roll(centre, span_z - 1, 1)
    return total


def transport_kernel(batches, place_ref, pop_ref, below_ref, above_ref, coef_ref, *rest):
    outs, (first, second, third) = rest[:batches], rest[batches:]
    bins, span_x, span_y, span_z = pop_ref.shape
    zeros = jnp.zeros((bins, span_z), jnp.float32)
    for ref in (first, second, third):
        for x in range(ref.shape[0]):
            ref[x, 0] = zeros
            ref[x, span_y + 1] = zeros
    for x in range(span_x):

        def fill(y, carry, x=x):
            first[x, y + 1] = decode(below_ref[x, y])
            first[span_x + x, y + 1] = cells_first(pop_ref, x, y, bins, span_x, span_y) * SCALE
            first[2 * span_x + x, y + 1] = decode(above_ref[x, y])
            return carry

        lax.fori_loop(0, span_y, fill, 0, unroll=2)
    for src, dst, shift in ((first, second, 0), (second, third, 1)):

        def layer(x, carry, src=src, dst=dst, shift=shift):
            def row(y, carry):
                dst[x, y + 1] = stencil(src, coef_ref, x, y, shift)
                return carry

            return lax.fori_loop(0, span_y, row, carry, unroll=4)

        lax.fori_loop(0, dst.shape[0], layer, 0)
    span_out = span_y // batches
    for ahead in range(batches):
        begin = lax.rem(place_ref[0] + ahead, batches) * span_out

        def layer(x, carry, ahead=ahead, begin=begin):
            for y in range(span_out):
                outs[ahead][x, y] = encode(stencil(third, coef_ref, x, begin + y, 2))
            return carry

        lax.fori_loop(0, span_x, layer, 0)


def transported(place, population, below, above, coefs, index, batches):
    _, span_x, span_y, span_z = population.shape
    out = (span_x, span_y // batches, GROUP, span_z)
    whole = lambda shape: pl.BlockSpec(shape, lambda i, place_ref: (0,) * len(shape))
    grid_spec = pltpu.PrefetchScalarGridSpec(
        num_scalar_prefetch=1,
        grid=(1,),
        in_specs=[
            pl.BlockSpec(
                (GROUP, span_x, span_y, span_z), lambda i, place_ref: (index, 0, 0, 0)
            ),
            whole(below.shape),
            whole(above.shape),
            whole(coefs.shape),
        ],
        out_specs=[whole(out)] * batches,
        scratch_shapes=[
            pltpu.VMEM((layers, span_y + 2, GROUP, span_z), jnp.float32)
            for layers in (3 * span_x, 3 * span_x - 2, 3 * span_x - 4)
        ],
    )
    return pl.pallas_call(
        functools.partial(transport_kernel, batches),
        grid_spec=grid_spec,
        out_shape=[jax.ShapeDtypeStruct(out, jnp.bfloat16)] * batches,
        compiler_params=params(),
        name="transport",
    )(place, population, below, above, coefs)


def table_kernel(kernel_ref, toeplitz_ref, column_ref):
    bin_count = toeplitz_ref.shape[0]
    wide = jnp.broadcast_to(kernel_ref[...], (bin_count, 2 * bin_count))
    turned = pltpu.roll(wide, 0, 1, stride=1, stride_axis=0)[:, :bin_count]
    column_ref[...] = jnp.broadcast_to(
        jnp.sum(turned, axis=1, keepdims=True), column_ref.shape
    )
    toeplitz_ref[...] = turned.T.astype(jnp.bfloat16)


def tables(kernel):
    bin_count = kernel.shape[0]
    return pl.pallas_call(
        table_kernel,
        in_specs=[vmem_spec()],
        out_specs=[vmem_spec()] * 2,
        out_shape=[
            jax.ShapeDtypeStruct((bin_count, bin_count), jnp.bfloat16),
            jax.ShapeDtypeStruct((bin_count, 128), jnp.float32),
        ],
        compiler_params=params(),
        name="tables",
    )(jnp.concatenate([kernel, jnp.zeros_like(kernel)])[None, :])


def kinetics_kernel(
    batches, groups, native, place_ref, supersat_ref, toeplitz_ref, column_ref, *rest
):
    parts = rest[: batches * groups]
    out_ref, depletion_ref, initial, even, odd = rest[batches * groups :]
    bin_count, width = initial.shape
    span_y, span_z = supersat_ref.shape[1:]
    pad = even.shape[0] - bin_count
    block = min(width, 2 * span_z)
    for ref in (even, odd):
        ref[0:pad, :] = jnp.zeros((pad, width), jnp.float32)
    for back in range(batches):
        source = lax.rem(place_ref[0] + batches - back, batches) * (groups * GROUP)
        for index in range(groups):
            part = parts[back * groups + index]
            at = pl.multiple_of(source + index * GROUP, GROUP)
            for y in range(span_y):
                value = decode(part[0, y]) * (1.0 / SCALE)
                cells = slice(y * span_z, (y + 1) * span_z)
                initial[pl.ds(at, GROUP), cells] = value
                even[pl.ds(pad + at, GROUP), cells] = value

    def substep(src, dst):
        for begin in range(0, width, block):
            cells = slice(begin, begin + block)
            speed = jnp.concatenate(
                [
                    supersat_ref[0, pl.ds(y, 1), :]
                    for y in range(begin // span_z, (begin + block) // span_z)
                ],
                axis=1,
            )
            column = jnp.concatenate([column_ref[...]] * (block // 128), axis=1)
            now = src[pad:, cells]
            product = jnp.dot(
                toeplitz_ref[...],
                now.astype(jnp.bfloat16),
                preferred_element_type=jnp.float32,
            )
            lower = src[pad - 1 : pad - 1 + bin_count, cells]
            change = (GROW / BETA) * (lower - now) + (product - column * now)
            dst[pad:, cells] = now + (BETA * speed) * change

    def pair(index, carry):
        substep(even, odd)
        substep(odd, even)
        return carry

    lax.fori_loop(0, KSTEPS // 2, pair, 0)
    bins = lax.broadcasted_iota(jnp.int32, (bin_count, span_z), 0).astype(jnp.float32)
    ratio = (bins + 1.0) / bin_count
    masses = ratio * ratio * ratio
    for y in range(span_y):
        cells = slice(y * span_z, (y + 1) * span_z)
        final = even[pad:, cells]
        depletion_ref[0, pl.ds(y, 1), :] = jnp.sum(
            masses * (final - initial[:, cells]), axis=0, keepdims=True
        )
        if native:
            rows = out_ref.reshape(bin_count * span_y, span_z)
            rows[pl.ds(y, bin_count, stride=span_y), :] = final
        else:
            out_ref[0, y] = final


def kinetics(place, supersat, toeplitz, column, parts, batches, groups):
    span_x, span_y, span_z = supersat.shape
    bin_count = toeplitz.shape[0]
    native = span_y % 8 == 0
    whole = lambda shape: pl.BlockSpec(shape, lambda i, place_ref: (0,) * len(shape))
    layer = lambda shape: pl.BlockSpec(
        (1,) + shape[1:], lambda i, place_ref: (i,) + (0,) * (len(shape) - 1)
    )
    if native:
        out_shape = (bin_count, span_x, span_y, span_z)
        out_spec = pl.BlockSpec(
            (bin_count, 1, span_y, span_z), lambda i, place_ref: (0, i, 0, 0)
        )
    else:
        out_shape = (span_x, span_y, bin_count, span_z)
        out_spec = layer(out_shape)
    grid_spec = pltpu.PrefetchScalarGridSpec(
        num_scalar_prefetch=1,
        grid=(span_x,),
        in_specs=[layer(supersat.shape), whole(toeplitz.shape), whole(column.shape)]
        + [layer(part.shape) for part in parts],
        out_specs=[out_spec, layer(supersat.shape)],
        scratch_shapes=[
            pltpu.VMEM((bin_count + pad, span_y * span_z), jnp.float32) for pad in (0, 8, 8)
        ],
    )
    out, depletion = pl.pallas_call(
        functools.partial(kinetics_kernel, batches, groups, native),
        grid_spec=grid_spec,
        out_shape=[
            jax.ShapeDtypeStruct(out_shape, jnp.float32),
            jax.ShapeDtypeStruct(supersat.shape, jnp.float32),
        ],
        compiler_params=params(),
        name="kinetics",
    )(place, supersat, toeplitz, column, *parts)
    return (out if native else jnp.transpose(out, (2, 0, 1, 3)), depletion)


def along(array, axis, by, around=False):
    count = lax.axis_size(axis)
    pairs = [(i, (i + by) % count) for i in range(count) if around or 0 <= i + by < count]
    return lax.ppermute(array, axis, pairs)


def weights(velocity):
    below = along(velocity, "space", 1)
    above = along(velocity, "space", -1)
    span_x = velocity.shape[1]
    vel = jnp.concatenate([below, velocity, above], axis=1).astype(jnp.float32)
    rise = COURANT * jnp.maximum(vel, 0.0)
    fall = -COURANT * jnp.minimum(vel, 0.0)

    def following(values, axis):
        sides = [(0, 0)] * 3
        sides[axis] = (0, 1)
        return lax.slice_in_dim(
            jnp.pad(values, sides), 1, values.shape[axis] + 1, axis=axis
        )

    here = slice(1, -1)
    rise_next = [following(rise[axis], axis)[here] for axis in range(3)]
    fall_next = [following(fall[axis], axis)[here] for axis in range(3)]
    rise, fall = rise[:, here], fall[:, here]
    kept = 1.0 - sum(rise_next) - fall[0] - fall[1] - fall[2]
    inner = (jnp.arange(vel.shape[3]) > 0).astype(jnp.float32)
    stacked = jnp.stack(
        [
            kept,
            rise[0],
            fall_next[0],
            rise[1],
            fall_next[1],
            rise[2] * inner,
            fall_next[2],
            jnp.zeros_like(kept),
        ],
        axis=2,
    )
    layers = jnp.arange(1, 3 * span_x - 1)
    exists = (layers >= span_x) | (lax.axis_index("space") > 0)
    return jnp.where(exists[:, None, None, None], stacked, 0.0)


def body(population, velocity, supersat, kernel):
    batches = lax.axis_size("bins")
    groups = population.shape[0] // GROUP
    place = lax.axis_index("bins").astype(jnp.int32)[None]
    coefs = weights(velocity)
    toeplitz, column = tables(kernel)
    codes = [coded_slab(population, index) for index in range(groups)]
    rims = [(along(code, "space", 1), along(code, "space", -1)) for code in codes]
    parts = [[None] * groups for _ in range(batches)]
    for index in range(groups):
        below, above = rims[index]
        pieces = transported(place, population, below, above, coefs, index, batches)
        for ahead in range(batches):
            piece = pieces[ahead]
            parts[ahead][index] = along(piece, "bins", ahead, True) if ahead else piece
    flat = [part for row in parts for part in row]
    new_population, depletion = kinetics(
        place, supersat, toeplitz, column, flat, batches, groups
    )
    depletion = lax.all_gather(depletion, "bins", axis=1, tiled=True)
    return (new_population, depletion)


def solution(mesh):
    in_specs = (
        P("bins", "space", None, None),
        P(None, "space", None, None),
        P("space", "bins", None),
        P(),
    )
    out_specs = (P(None, "space", "bins", None), P("space", None, None))
    return jax.shard_map(body, mesh=mesh, in_specs=in_specs, out_specs=out_specs, check_vma=False)
```

```python
import functools

import jax
import jax.numpy as jnp
from jax import lax
from jax.experimental import pallas as pl
from jax.experimental.pallas import tpu as pltpu
from jax.sharding import PartitionSpec as P

STEPS = 3
KSTEPS = 8

COURANT = 0.3
GROW = 0.4
BETA = 0.5

POWER = 9
SCALE = 256.0
GROUP = 16
VMEM_LIMIT = 32 * 1024 * 1024


def encode(scaled):
    square = scaled * scaled
    fourth = square * square
    return (fourth * fourth * scaled).astype(jnp.bfloat16)


def decode(code):
    wide = code.astype(jnp.float32)
    size = jnp.exp(jnp.log(jnp.abs(wide)) * (1.0 / POWER))
    return jnp.where(wide < 0.0, -size, size)


def params(limit=VMEM_LIMIT):
    return pltpu.CompilerParams(vmem_limit_bytes=limit)


def cost(flops, size):
    return pl.CostEstimate(flops=flops, bytes_accessed=size, transcendentals=0)


def vmem_spec():
    return pl.BlockSpec(memory_space=pltpu.VMEM)


def smem_spec():
    return pl.BlockSpec(memory_space=pltpu.SMEM)


def code_kernel(pop_ref, velocity_ref, all_ref, *group_refs):
    bins = pop_ref.shape[0]
    all_ref[pl.ds(bins, 3)] = velocity_ref[...]
    all_ref[pl.ds(bins + 3, GROUP - 3)] = jnp.zeros(
        (GROUP - 3,) + all_ref.shape[1:], jnp.bfloat16
    )
    group_refs[0][pl.ds(GROUP, 3)] = velocity_ref[...]

    for number, group_ref in enumerate(group_refs):

        def layer(x, carry, number=number, group_ref=group_ref):
            for index in range(0, GROUP, 4):
                code = encode(pop_ref[pl.ds(number * GROUP + index, 4), x] * SCALE)
                all_ref[pl.ds(number * GROUP + index, 4), x] = code
                group_ref[pl.ds(index, 4), x] = code
            return carry

        lax.fori_loop(0, pop_ref.shape[1], layer, 0)


def coded_slab(population, velocity):
    bins = population.shape[0]
    span = population.shape[1:]
    groups = bins // GROUP
    sizes = [bins + GROUP, GROUP + 3] + [GROUP] * (groups - 1)
    return pl.pallas_call(
        code_kernel,
        in_specs=[vmem_spec()] * 2,
        out_specs=[vmem_spec()] * len(sizes),
        out_shape=[jax.ShapeDtypeStruct((size,) + span, jnp.bfloat16) for size in sizes],
        compiler_params=params(),
        cost_estimate=cost(0, 6_000_000),
        name="code_slab",
    )(population, velocity)


def weight_kernel(place_ref, own_ref, inside_ref, outside_ref, coef_ref, vel_ref):
    _, span_x, span_y, span_z = own_ref.shape
    odd = lax.rem(place_ref[1], 2)
    inside = 2 * span_x * (1 - odd)
    for axis in range(3):
        for x in range(span_x):
            vel_ref[axis, inside + x] = inside_ref[axis, x].astype(jnp.float32)
            vel_ref[axis, span_x + x] = own_ref[axis, x].astype(jnp.float32)
            vel_ref[axis, 2 * span_x - inside + x] = outside_ref[GROUP + axis, x].astype(jnp.float32)
    rows = lax.broadcasted_iota(jnp.int32, (span_y, span_z), 0)
    lanes = lax.broadcasted_iota(jnp.int32, (span_y, span_z), 1)

    def layer(x, carry):
        kept_in = jnp.where((x + 1 >= span_x) | (place_ref[1] > 0), 1.0, 0.0)
        scale = COURANT * kept_in
        rise = lambda value: jnp.maximum(value, 0.0) * scale
        fall = lambda value: jnp.minimum(value, 0.0) * (-scale)
        vel_x, next_x = vel_ref[0, x + 1], vel_ref[0, x + 2]
        vel_y, vel_z = vel_ref[1, x + 1], vel_ref[2, x + 1]
        next_y = jnp.where(rows < span_y - 1, pltpu.roll(vel_y, span_y - 1, 0), 0.0)
        next_z = jnp.where(lanes < span_z - 1, pltpu.roll(vel_z, span_z - 1, 1), 0.0)
        coef_ref[0, x] = kept_in - (
            rise(next_x) + fall(vel_x) + rise(next_y) + fall(vel_y) + rise(next_z) + fall(vel_z)
        )
        coef_ref[1, x] = rise(vel_x)
        coef_ref[2, x] = fall(next_x)
        coef_ref[3, x] = rise(vel_y)
        coef_ref[4, x] = fall(next_y)
        coef_ref[5, x] = jnp.where(lanes > 0, rise(vel_z), 0.0)
        coef_ref[6, x] = fall(next_z)
        return carry

    lax.fori_loop(0, coef_ref.shape[1], layer, 0)


def weights(place, velocity, inside, outside):
    span = velocity.shape[1:]
    whole = lambda shape: pl.BlockSpec(shape, lambda i: (0, 0, 0, 0))
    tail = inside.shape[0] // GROUP - 1
    return pl.pallas_call(
        weight_kernel,
        grid=(1,),
        in_specs=[
            smem_spec(),
            whole(velocity.shape),
            pl.BlockSpec((GROUP,) + span, lambda i: (tail, 0, 0, 0)),
            whole(outside.shape),
        ],
        out_specs=whole((7, 3 * span[0] - 2) + span[1:]),
        out_shape=jax.ShapeDtypeStruct((7, 3 * span[0] - 2) + span[1:], jnp.float32),
        scratch_shapes=[pltpu.VMEM((3, 3 * span[0]) + span[1:], jnp.float32)],
        compiler_params=params(),
        cost_estimate=cost(0, 4_000_000),
        name="weights",
    )(place, velocity, inside, outside)


RIM = 8


def transport_kernel(batches, place_ref, pop_ref, inside_ref, outside_ref, coef_ref, *rest):
    *outs, first, second, third, last = rest[-batches - 4 :]
    _, span_x, span_y, span_z = pop_ref.shape
    bins = GROUP
    zeros = jnp.zeros((bins, RIM, span_z), jnp.float32)
    for ref in (first, second, third):
        for x in range(ref.shape[0]):
            ref[x, :, pl.ds(0, RIM)] = zeros
            ref[x, :, pl.ds(RIM + span_y, RIM)] = zeros
    inside = 2 * span_x * (1 - lax.rem(place_ref[1], 2))
    body = pl.ds(RIM, span_y)

    def fill(x, carry):
        for index in range(bins):
            first[inside + x, index, body] = decode(inside_ref[index, x])
            first[span_x + x, index, body] = pop_ref[index, x] * SCALE
            first[2 * span_x - inside + x, index, body] = decode(outside_ref[index, x])
        return carry

    lax.fori_loop(0, span_x, fill, 0)

    for src, dst, shift, rim in (
        (first, second, 0, RIM),
        (second, third, 1, RIM),
        (third, last, 2, 0),
    ):

        def layer(x, carry, src=src, dst=dst, shift=shift, rim=rim):
            for y in range(0, span_y, 8):
                here, down, up = (pl.ds(RIM + y + by, 8) for by in (0, -1, 1))
                weight = [coef_ref[k, x + shift, pl.ds(y, 8)] for k in range(7)]
                for index in range(bins):
                    centre = src[x + 1, index, here]
                    total = weight[0] * centre
                    total += weight[1] * src[x, index, here]
                    total += weight[2] * src[x + 2, index, here]
                    total += weight[3] * src[x + 1, index, down]
                    total += weight[4] * src[x + 1, index, up]
                    total += weight[5] * pltpu.roll(centre, 1, 1)
                    total += weight[6] * pltpu.roll(centre, span_z - 1, 1)
                    dst[x, index, pl.ds(rim + y, 8)] = total
            return carry

        lax.fori_loop(0, dst.shape[0], layer, 0)
    span_out = span_y // batches
    rows = last.reshape(span_x * bins * span_y, span_z)
    for ahead in range(batches):
        begin = lax.bitwise_xor(place_ref[0], ahead) * span_out
        for x in range(span_x):
            for y in range(span_out):
                at = x * bins * span_y + begin + y
                outs[ahead][x, y] = encode(rows[pl.ds(at, bins, stride=span_y), :])


def transported(place, population, inside, outside, coefs, group, batches, after):
    _, span_x, span_y, span_z = population.shape
    out = (span_x, span_y // batches, GROUP, span_z)
    block = (GROUP, span_x, span_y, span_z)
    at = lambda shape, start: pl.BlockSpec(shape, lambda i: (start, 0, 0, 0))
    return pl.pallas_call(
        functools.partial(transport_kernel, batches),
        grid=(1,),
        in_specs=[smem_spec(), at(block, group), at(block, group), at(block, 0), at(coefs.shape, 0)]
        + [pl.BlockSpec(memory_space=pl.ANY)] * len(after),
        out_specs=[at(out, 0)] * batches,
        out_shape=[jax.ShapeDtypeStruct(out, jnp.bfloat16)] * batches,
        scratch_shapes=[
            pltpu.VMEM((depth, GROUP, span_y + 2 * RIM, span_z), jnp.float32)
            for depth in (3 * span_x, 3 * span_x - 2, 3 * span_x - 4)
        ]
        + [pltpu.VMEM((span_x, GROUP, span_y, span_z), jnp.float32)],
        compiler_params=params(),
        cost_estimate=cost(0, 18_000_000),
        name="transport",
    )(place, population, inside, outside, coefs, *after)


def bins_of_rows(shape, dim):
    count = shape[dim]
    row = lax.broadcasted_iota(jnp.int32, shape, dim)
    return (row % 8) * (count // 8) + row // 8


def table_kernel(kernel_ref, toeplitz_ref, column_ref):
    bin_count = toeplitz_ref.shape[0]
    square = (bin_count, bin_count)
    wide = jnp.broadcast_to(kernel_ref[...], (bin_count, 2 * bin_count))
    turned = pltpu.roll(wide, 0, 1, stride=1, stride_axis=0)[:, :bin_count]
    column = jnp.broadcast_to(jnp.sum(turned, axis=1, keepdims=True), column_ref.shape)
    plain = turned.T.astype(jnp.bfloat16)
    other = lax.broadcasted_iota(jnp.int32, square, 1)
    moves = jnp.where(bins_of_rows(square, 0) == other, 1.0, 0.0)
    exact = functools.partial(
        jnp.dot, preferred_element_type=jnp.float32, precision=lax.Precision.HIGHEST
    )
    column_ref[...] = exact(moves, column) + GROW / BETA
    moves = moves.astype(jnp.bfloat16)
    half = jnp.dot(moves, plain, preferred_element_type=jnp.float32).astype(jnp.bfloat16)
    toeplitz_ref[...] = jnp.dot(half, moves.T, preferred_element_type=jnp.float32).astype(
        jnp.bfloat16
    )


def tables(kernel):
    bin_count = kernel.shape[0]
    return pl.pallas_call(
        table_kernel,
        in_specs=[vmem_spec()],
        out_specs=[vmem_spec()] * 2,
        out_shape=[
            jax.ShapeDtypeStruct((bin_count, bin_count), jnp.bfloat16),
            jax.ShapeDtypeStruct((bin_count, 128), jnp.float32),
        ],
        compiler_params=params(),
        name="tables",
    )(jnp.concatenate([kernel, jnp.zeros_like(kernel)])[None, :])


def kinetics_kernel(
    batches, groups, layer, native, chained, place_ref, supersat_ref, toeplitz_ref, column_ref, *rest
):
    parts = rest[: batches * groups]
    out_ref, depletion_ref, initial, state, product, rounded = rest[batches * groups + chained :]
    bin_count, width = state.shape
    span_y, span_z = supersat_ref.shape[1:]
    run = bin_count // 8
    block = min(width, 2 * span_z)
    for back in range(batches):
        source = lax.bitwise_xor(place_ref[0], back) * (groups * GROUP)
        for index in range(groups):
            part = parts[back * groups + index]
            begin = source + index * GROUP
            at = lax.rem(begin, run) * 8 + begin // run
            for y in range(span_y):
                value = decode(part[layer, y]) * (1.0 / SCALE)
                initial[pl.ds(y * bin_count + at, GROUP, stride=8), :] = value
    for y in range(span_y):
        cells = slice(y * span_z, (y + 1) * span_z)
        for row in range(0, bin_count, 16):
            value = initial[pl.ds(y * bin_count + row, 16), :]
            state[pl.ds(row, 16), cells] = value
            rounded[pl.ds(row, 16), cells] = value.astype(jnp.bfloat16)

    eighth = lax.broadcasted_iota(jnp.int32, (8, span_z), 0)

    def multiply(begin):
        cells = slice(begin, begin + block)
        product[:, cells] = jnp.dot(
            toeplitz_ref[...], rounded[:, cells], preferred_element_type=jnp.float32
        )

    def advance(begin):
        lanes = [slice(lane, lane + span_z) for lane in range(begin, begin + block, span_z)]
        speeds, lowers = [], []
        for cells in lanes:
            row = supersat_ref[layer, pl.ds(cells.start // span_z, 1), :]
            speeds.append(BETA * jnp.broadcast_to(row, (8, span_z)))
            last = state[pl.ds(bin_count - 8, 8), cells]
            lowers.append(jnp.where(eighth > 0, pltpu.roll(last, 1, 0), 0.0))
        for row in range(0, bin_count, 16):
            pairs = [[] for _ in lanes]
            for at in (pl.ds(row, 8), pl.ds(row + 8, 8)):
                column = column_ref[at, :]
                for index, cells in enumerate(lanes):
                    now = state[at, cells]
                    change = (GROW / BETA) * lowers[index] - column * now
                    new = now + speeds[index] * (change + product[at, cells])
                    state[at, cells] = new
                    pairs[index].append(new)
                    lowers[index] = now
            for pair, cells in zip(pairs, lanes):
                rounded[pl.ds(row, 16), cells] = jnp.concatenate(pair, axis=0).astype(
                    jnp.bfloat16
                )

    def substep(index, carry):
        begins = list(range(0, width, block))
        multiply(begins[0])
        for begin, following in zip(begins, begins[1:] + [None]):
            if following is not None:
                multiply(following)
            advance(begin)
        return carry

    lax.fori_loop(0, KSTEPS, substep, 0)
    ratio = (bins_of_rows((bin_count, span_z), 0).astype(jnp.float32) + 1.0) / bin_count
    masses = ratio * ratio * ratio
    for y in range(span_y):
        cells = slice(y * span_z, (y + 1) * span_z)
        final = state[:, cells]
        depletion_ref[0, pl.ds(y, 1), :] = jnp.sum(
            masses * (final - initial[pl.ds(y * bin_count, bin_count), :]), axis=0, keepdims=True
        )
        if native:
            rows = out_ref.reshape(bin_count * span_y, span_z)
        for row in range(run):
            value = state[pl.ds(8 * row, 8), cells]
            if native:
                rows[pl.ds(row * span_y + y, 8, stride=run * span_y), :] = value
            else:
                out_ref[0, y, pl.ds(row, 8, stride=run), :] = value


def kinetics(place, supersat, toeplitz, column, parts, layer, batches, chain):
    span_x, span_y, span_z = supersat.shape
    bin_count = toeplitz.shape[0]
    native = span_y % 8 == 0
    whole = pl.BlockSpec(memory_space=pltpu.VMEM)
    if native:
        out_shape = (bin_count, span_x, span_y, span_z)
        out_spec = pl.BlockSpec((bin_count, 1, span_y, span_z), lambda i: (0, layer, 0, 0))
    else:
        out_shape = (span_x, span_y, bin_count, span_z)
        out_spec = pl.BlockSpec((1,) + out_shape[1:], lambda i: (layer, 0, 0, 0))
    chained = 0 if chain is None else 1
    return pl.pallas_call(
        functools.partial(kinetics_kernel, batches, len(parts) // batches, layer, native, chained),
        grid=(1,),
        in_specs=[smem_spec()]
        + [whole] * (3 + len(parts))
        + [pl.BlockSpec(memory_space=pl.ANY)] * chained,
        out_specs=[out_spec, whole],
        out_shape=[
            jax.ShapeDtypeStruct(out_shape, jnp.float32),
            jax.ShapeDtypeStruct((1, span_y, span_z), jnp.float32),
        ],
        scratch_shapes=[
            pltpu.VMEM((bin_count * span_y, span_z), jnp.float32),
            pltpu.VMEM((bin_count, span_y * span_z), jnp.float32),
            pltpu.VMEM((bin_count, span_y * span_z), jnp.float32),
            pltpu.VMEM((bin_count, span_y * span_z), jnp.bfloat16),
        ],
        input_output_aliases={4 + len(parts): 0} if chained else {},
        compiler_params=params(),
        cost_estimate=cost(0, 22_000_000),
        name="kinetics",
    )(place, supersat, toeplitz, column, *parts, *([chain] if chained else []))


def assemble_kernel(batches, place_ref, *refs):
    *parts, out_ref = refs
    for back in range(batches):
        source = lax.bitwise_xor(place_ref[0], back)
        for layer in range(out_ref.shape[0]):
            out_ref[layer, source] = parts[back][layer]


def assembled(place, parts, batches):
    span_x, span_y, span_z = parts[0].shape
    out = pl.pallas_call(
        functools.partial(assemble_kernel, batches),
        in_specs=[pl.BlockSpec(memory_space=pltpu.SMEM)] + [vmem_spec()] * batches,
        out_specs=vmem_spec(),
        out_shape=jax.ShapeDtypeStruct((span_x, batches, span_y, span_z), jnp.float32),
        compiler_params=params(),
        name="assemble",
    )(place, *parts)
    return out.reshape(span_x, batches * span_y, span_z)


def swapped(array, axis, partner):
    count = lax.axis_size(axis)
    pairs = [(i, partner(i)) for i in range(count) if 0 <= partner(i) < count]
    return lax.ppermute(array, axis, pairs)


def with_partner(array):
    return swapped(array, "space", lambda i: i ^ 1)


def with_other(array):
    return swapped(array, "space", lambda i: ((i + 1) ^ 1) - 1)


def body(population, velocity, supersat, kernel):
    batches = lax.axis_size("bins")
    span_x = population.shape[1]
    place = jnp.stack([lax.axis_index("bins"), lax.axis_index("space")]).astype(jnp.int32)
    toeplitz, column = tables(kernel)
    codes, *groups = coded_slab(population, velocity)
    inside = with_partner(codes)
    outside = [with_other(group) for group in groups]
    coefs = weights(place, velocity, inside, outside[0])
    parts = [[] for _ in range(batches)]
    moved = []
    for group in range(len(groups)):
        after = list(moved[:1]) + ([row[group - 2] for row in parts[1:]] if group > 1 else [])
        moved = transported(
            place, population, inside, outside[group], coefs, group, batches, after
        )
        for ahead, array in enumerate(moved):
            if ahead:
                array = swapped(array, "bins", lambda i: i ^ ahead)
            parts[ahead].append(array)
    flat = [part for row in parts for part in row]
    out, depletions = None, []
    for layer in range(span_x):
        out, depletion = kinetics(
            place, supersat, toeplitz, column, flat, layer, batches, out
        )
        depletions.append(depletion)
    if not supersat.shape[1] % 8 == 0:
        out = jnp.transpose(out, (2, 0, 1, 3))
    own = jnp.concatenate(depletions, axis=0)
    others = [own] + [swapped(own, "bins", lambda i: i ^ ahead) for ahead in range(1, batches)]
    return (out, assembled(place, others, batches))


def solution(mesh):
    in_specs = (
        P("bins", "space", None, None),
        P(None, "space", None, None),
        P("space", "bins", None),
        P(),
    )
    out_specs = (P(None, "space", "bins", None), P("space", None, None))
    return jax.shard_map(body, mesh=mesh, in_specs=in_specs, out_specs=out_specs, check_vma=False)
```

```python
import functools

import jax
import jax.numpy as jnp
from jax import lax
from jax.experimental import pallas as pl
from jax.experimental.pallas import tpu as pltpu
from jax.sharding import PartitionSpec as P

STEPS = 3
KSTEPS = 8

COURANT = 0.3
GROW = 0.4
BETA = 0.5

POWER = 9
SCALE = 256.0
GROUP = 16
VMEM_LIMIT = 32 * 1024 * 1024


def encode(scaled):
    square = scaled * scaled
    fourth = square * square
    return (fourth * fourth * scaled).astype(jnp.bfloat16)


def decode(code):
    wide = code.astype(jnp.float32)
    size = jnp.exp(jnp.log(jnp.abs(wide)) * (1.0 / POWER))
    return jnp.where(wide < 0.0, -size, size)


def params(limit=VMEM_LIMIT):
    return pltpu.CompilerParams(vmem_limit_bytes=limit)


def cost(flops, size):
    return pl.CostEstimate(flops=flops, bytes_accessed=size, transcendentals=0)


def vmem_spec():
    return pl.BlockSpec(memory_space=pltpu.VMEM)


def smem_spec():
    return pl.BlockSpec(memory_space=pltpu.SMEM)


def code_kernel(pop_ref, velocity_ref, all_ref, *group_refs):
    bins = pop_ref.shape[0]
    all_ref[pl.ds(bins, 3)] = velocity_ref[...]
    all_ref[pl.ds(bins + 3, GROUP - 3)] = jnp.zeros(
        (GROUP - 3,) + all_ref.shape[1:], jnp.bfloat16
    )
    group_refs[0][pl.ds(GROUP, 3)] = velocity_ref[...]

    for number, group_ref in enumerate(group_refs):

        def layer(x, carry, number=number, group_ref=group_ref):
            for index in range(0, GROUP, 4):
                code = encode(pop_ref[pl.ds(number * GROUP + index, 4), x] * SCALE)
                all_ref[pl.ds(number * GROUP + index, 4), x] = code
                group_ref[pl.ds(index, 4), x] = code
            return carry

        lax.fori_loop(0, pop_ref.shape[1], layer, 0)


def coded_slab(population, velocity):
    bins = population.shape[0]
    span = population.shape[1:]
    groups = bins // GROUP
    sizes = [bins + GROUP, GROUP + 3] + [GROUP] * (groups - 1)
    return pl.pallas_call(
        code_kernel,
        in_specs=[vmem_spec()] * 2,
        out_specs=[vmem_spec()] * len(sizes),
        out_shape=[jax.ShapeDtypeStruct((size,) + span, jnp.bfloat16) for size in sizes],
        compiler_params=params(),
        cost_estimate=cost(0, 6_000_000),
        name="code_slab",
    )(population, velocity)


def weight_kernel(place_ref, own_ref, inside_ref, outside_ref, coef_ref, vel_ref):
    _, span_x, span_y, span_z = own_ref.shape
    odd = lax.rem(place_ref[1], 2)
    inside = 2 * span_x * (1 - odd)
    for axis in range(3):
        for x in range(span_x):
            vel_ref[axis, inside + x] = inside_ref[axis, x].astype(jnp.float32)
            vel_ref[axis, span_x + x] = own_ref[axis, x].astype(jnp.float32)
            vel_ref[axis, 2 * span_x - inside + x] = outside_ref[GROUP + axis, x].astype(jnp.float32)
    rows = lax.broadcasted_iota(jnp.int32, (span_y, span_z), 0)
    lanes = lax.broadcasted_iota(jnp.int32, (span_y, span_z), 1)

    def layer(x, carry):
        kept_in = jnp.where((x + 1 >= span_x) | (place_ref[1] > 0), 1.0, 0.0)
        scale = COURANT * kept_in
        rise = lambda value: jnp.maximum(value, 0.0) * scale
        fall = lambda value: jnp.minimum(value, 0.0) * (-scale)
        vel_x, next_x = vel_ref[0, x + 1], vel_ref[0, x + 2]
        vel_y, vel_z = vel_ref[1, x + 1], vel_ref[2, x + 1]
        next_y = jnp.where(rows < span_y - 1, pltpu.roll(vel_y, span_y - 1, 0), 0.0)
        next_z = jnp.where(lanes < span_z - 1, pltpu.roll(vel_z, span_z - 1, 1), 0.0)
        coef_ref[0, x] = kept_in - (
            rise(next_x) + fall(vel_x) + rise(next_y) + fall(vel_y) + rise(next_z) + fall(vel_z)
        )
        coef_ref[1, x] = rise(vel_x)
        coef_ref[2, x] = fall(next_x)
        coef_ref[3, x] = rise(vel_y)
        coef_ref[4, x] = fall(next_y)
        coef_ref[5, x] = jnp.where(lanes > 0, rise(vel_z), 0.0)
        coef_ref[6, x] = fall(next_z)
        return carry

    lax.fori_loop(0, coef_ref.shape[1], layer, 0)


def weights(place, velocity, inside, outside):
    span = velocity.shape[1:]
    whole = lambda shape: pl.BlockSpec(shape, lambda i: (0, 0, 0, 0))
    tail = inside.shape[0] // GROUP - 1
    return pl.pallas_call(
        weight_kernel,
        grid=(1,),
        in_specs=[
            smem_spec(),
            whole(velocity.shape),
            pl.BlockSpec((GROUP,) + span, lambda i: (tail, 0, 0, 0)),
            whole(outside.shape),
        ],
        out_specs=whole((7, 3 * span[0] - 2) + span[1:]),
        out_shape=jax.ShapeDtypeStruct((7, 3 * span[0] - 2) + span[1:], jnp.float32),
        scratch_shapes=[pltpu.VMEM((3, 3 * span[0]) + span[1:], jnp.float32)],
        compiler_params=params(),
        cost_estimate=cost(0, 4_000_000),
        name="weights",
    )(place, velocity, inside, outside)


RIM = 8
PIECE = 32


def transport_kernel(batches, place_ref, pop_ref, inside_ref, outside_ref, coef_ref, *rest):
    *outs, first, second, third, last = rest[-batches - 4 :]
    _, span_x, span_y, span_z = pop_ref.shape
    bins = GROUP
    zeros = jnp.zeros((bins, RIM, span_z), jnp.float32)
    for ref in (first, second, third):
        for x in range(ref.shape[0]):
            ref[x, :, pl.ds(0, RIM)] = zeros
            ref[x, :, pl.ds(RIM + span_y, RIM)] = zeros
    inside = 2 * span_x * (1 - lax.rem(place_ref[1], 2))
    body = pl.ds(RIM, span_y)

    def fill(x, carry):
        for index in range(bins):
            first[inside + x, index, body] = decode(inside_ref[index, x])
            first[span_x + x, index, body] = pop_ref[index, x] * SCALE
            first[2 * span_x - inside + x, index, body] = decode(outside_ref[index, x])
        return carry

    lax.fori_loop(0, span_x, fill, 0)

    for src, dst, shift, rim in (
        (first, second, 0, RIM),
        (second, third, 1, RIM),
        (third, last, 2, 0),
    ):

        def layer(x, carry, src=src, dst=dst, shift=shift, rim=rim):
            for y in range(0, span_y, 8):
                here, down, up = (pl.ds(RIM + y + by, 8) for by in (0, -1, 1))
                weight = [coef_ref[k, x + shift, pl.ds(y, 8)] for k in range(7)]
                for index in range(bins):
                    centre = src[x + 1, index, here]
                    total = weight[0] * centre
                    total += weight[1] * src[x, index, here]
                    total += weight[2] * src[x + 2, index, here]
                    total += weight[3] * src[x + 1, index, down]
                    total += weight[4] * src[x + 1, index, up]
                    total += weight[5] * pltpu.roll(centre, 1, 1)
                    total += weight[6] * pltpu.roll(centre, span_z - 1, 1)
                    dst[x, index, pl.ds(rim + y, 8)] = total
            return carry

        lax.fori_loop(0, dst.shape[0], layer, 0)
    span_out = span_y // batches
    rows = last.reshape(span_x * bins * span_y, span_z)
    for ahead in range(batches):
        begin = lax.bitwise_xor(place_ref[0], ahead) * span_out
        for x in range(span_x):
            for y in range(span_out):
                at = x * bins * span_y + begin + y
                outs[ahead][x, y] = encode(rows[pl.ds(at, bins, stride=span_y), :])


def transported(place, population, inside, outside, coefs, group, batches, after):
    _, span_x, span_y, span_z = population.shape
    out = (span_x, span_y // batches, GROUP, span_z)
    block = (GROUP, span_x, span_y, span_z)
    at = lambda shape, start: pl.BlockSpec(shape, lambda i: (start, 0, 0, 0))
    return pl.pallas_call(
        functools.partial(transport_kernel, batches),
        grid=(1,),
        in_specs=[smem_spec(), at(block, group), at(block, group), at(block, 0), at(coefs.shape, 0)]
        + [pl.BlockSpec(memory_space=pl.ANY)] * len(after),
        out_specs=[at(out, 0)] * batches,
        out_shape=[jax.ShapeDtypeStruct(out, jnp.bfloat16)] * batches,
        scratch_shapes=[
            pltpu.VMEM((depth, GROUP, span_y + 2 * RIM, span_z), jnp.float32)
            for depth in (3 * span_x, 3 * span_x - 2, 3 * span_x - 4)
        ]
        + [pltpu.VMEM((span_x, GROUP, span_y, span_z), jnp.float32)],
        compiler_params=params(),
        cost_estimate=cost(0, 18_000_000),
        name="transport",
    )(place, population, inside, outside, coefs, *after)


def bins_of_rows(shape, dim):
    count = shape[dim]
    row = lax.broadcasted_iota(jnp.int32, shape, dim)
    return (row % 8) * (count // 8) + row // 8


def table_kernel(kernel_ref, toeplitz_ref, column_ref):
    bin_count = toeplitz_ref.shape[0]
    square = (bin_count, bin_count)
    wide = jnp.broadcast_to(kernel_ref[...], (bin_count, 2 * bin_count))
    turned = pltpu.roll(wide, 0, 1, stride=1, stride_axis=0)[:, :bin_count]
    column = jnp.broadcast_to(jnp.sum(turned, axis=1, keepdims=True), column_ref.shape)
    plain = turned.T.astype(jnp.bfloat16)
    other = lax.broadcasted_iota(jnp.int32, square, 1)
    moves = jnp.where(bins_of_rows(square, 0) == other, 1.0, 0.0)
    exact = functools.partial(
        jnp.dot, preferred_element_type=jnp.float32, precision=lax.Precision.HIGHEST
    )
    column_ref[...] = exact(moves, column) + GROW / BETA
    moves = moves.astype(jnp.bfloat16)
    half = jnp.dot(moves, plain, preferred_element_type=jnp.float32).astype(jnp.bfloat16)
    toeplitz_ref[...] = jnp.dot(half, moves.T, preferred_element_type=jnp.float32).astype(
        jnp.bfloat16
    )


def tables(kernel):
    bin_count = kernel.shape[0]
    return pl.pallas_call(
        table_kernel,
        in_specs=[vmem_spec()],
        out_specs=[vmem_spec()] * 2,
        out_shape=[
            jax.ShapeDtypeStruct((bin_count, bin_count), jnp.bfloat16),
            jax.ShapeDtypeStruct((bin_count, 128), jnp.float32),
        ],
        compiler_params=params(),
        name="tables",
    )(jnp.concatenate([kernel, jnp.zeros_like(kernel)])[None, :])


def unpack(place_ref, parts, first, groups, batches, bin_count, store):
    run = bin_count // 8
    count = len(parts) // batches
    for back in range(batches):
        source = lax.bitwise_xor(place_ref[0], back) * (groups * GROUP)
        for index in range(count):
            part = parts[back * count + index]
            begin = source + (first + index) * GROUP
            at = lax.rem(begin, run) * 8 + begin // run
            for y in range(part.shape[1]):
                value = decode(part[0, y]) * (1.0 / SCALE)
                store(pl.ds(y * bin_count + at, GROUP, stride=8), value)


def unpack_kernel(batches, groups, place_ref, *refs):
    *parts, out_ref = refs
    _, rows, span_z = out_ref.shape
    layer = out_ref.reshape(rows, span_z)

    def store(where, value):
        layer[where, :] = value

    unpack(place_ref, parts, 0, groups, batches, groups * GROUP * batches, store)


def layer_spec(shape):
    return pl.BlockSpec((1,) + shape[1:], lambda i: (i,) + (0,) * (len(shape) - 1))


def unpacked(place, parts, groups, batches):
    span_x, span_y, _, span_z = parts[0].shape
    shape = (span_x, span_y * groups * GROUP * batches, span_z)
    return pl.pallas_call(
        functools.partial(unpack_kernel, batches, groups),
        grid=(span_x,),
        in_specs=[smem_spec()] + [layer_spec(part.shape) for part in parts],
        out_specs=layer_spec(shape),
        out_shape=jax.ShapeDtypeStruct(shape, jnp.float32),
        compiler_params=params(),
        cost_estimate=cost(0, 12_000_000),
        name="unpack",
    )(place, *parts)


def kinetics_kernel(batches, groups, native, place_ref, supersat_ref, toeplitz_ref, column_ref, *rest):
    *parts, out_ref, depletion_ref, state = rest
    bin_count = toeplitz_ref.shape[0]
    span_y, span_z = supersat_ref.shape[1:]
    run = bin_count // 8
    tiles = bin_count // span_z
    count = span_y // tiles
    if groups > 1:
        *parts, early_ref = parts
        state[...] = early_ref[0]

    def store(where, value):
        state[where, :] = value

    unpack(place_ref, parts, groups - 1, groups, batches, bin_count, store)
    ratio = (bins_of_rows((bin_count, span_z), 0).astype(jnp.float32) + 1.0) / bin_count
    masses = ratio * ratio * ratio

    def mass(y):
        return jnp.sum(
            masses * state[pl.ds(y * bin_count, bin_count), :], axis=0, keepdims=True
        )

    for y in range(span_y):
        depletion_ref[0, pl.ds(y, 1), :] = mass(y)

    def steps(*sums):
        eighth = lax.broadcasted_iota(jnp.int32, (8, span_z), 0)
        pieces = bin_count // PIECE

        def multiply(number, rounded):
            stage = number // 2 % 2
            pltpu.matmul_push_rhs(rounded, stage, number % 2)
            for piece in range(pieces):
                pltpu.matmul_acc_lhs(
                    sums[number * pieces + piece],
                    toeplitz_ref[pl.ds(piece * PIECE, PIECE), :],
                    load_staged_rhs=None if piece else stage,
                )

        def advance(number):
            speeds, lowers = [], []
            for tile in range(tiles):
                y = number * tiles + tile
                row = supersat_ref[0, pl.ds(y, 1), :]
                speeds.append(BETA * jnp.broadcast_to(row, (8, span_z)))
                last = state[pl.ds((y + 1) * bin_count - 8, 8), :]
                lowers.append(jnp.where(eighth > 0, pltpu.roll(last, 1, 0), 0.0))
            rounded = []
            for row in range(0, bin_count, 16):
                if row % PIECE == 0:
                    product = pltpu.matmul_pop(sums[number * pieces + row // PIECE])
                pairs = [[] for _ in range(tiles)]
                for at in (row, row + 8):
                    column = column_ref[pl.ds(at, 8), :]
                    for tile in range(tiles):
                        where = pl.ds((number * tiles + tile) * bin_count + at, 8)
                        now = state[where, :]
                        change = (GROW / BETA) * lowers[tile] - column * now
                        change += product[
                            at % PIECE : at % PIECE + 8, tile * span_z : (tile + 1) * span_z
                        ]
                        new = now + speeds[tile] * change
                        state[where, :] = new
                        pairs[tile].append(new)
                        lowers[tile] = now
                rounded.append(
                    jnp.concatenate(
                        [jnp.concatenate(pair, axis=0) for pair in pairs], axis=1
                    ).astype(jnp.bfloat16)
                )
            return jnp.concatenate(rounded, axis=0)

        for number in range(count):
            values = [
                state[pl.ds((number * tiles + tile) * bin_count, bin_count), :]
                for tile in range(tiles)
            ]
            multiply(number, jnp.concatenate(values, axis=1).astype(jnp.bfloat16))

        def substep(index, carry):
            for number in range(count):
                multiply(number, advance(number))
            return carry

        lax.fori_loop(0, KSTEPS - 1, substep, 0)
        for number in range(count):
            advance(number)

    pl.run_scoped(
        steps,
        *(
            pltpu.ACC(mxu_id=number % 2)((PIECE, bin_count), jnp.float32)
            for number in range(count)
            for piece in range(bin_count // PIECE)
        ),
    )
    for y in range(span_y):
        depletion_ref[0, pl.ds(y, 1), :] = mass(y) - depletion_ref[0, pl.ds(y, 1), :]
        if native:
            rows = out_ref.reshape(bin_count * span_y, span_z)
        for row in range(run):
            value = state[pl.ds(y * bin_count + 8 * row, 8), :]
            if native:
                rows[pl.ds(row * span_y + y, 8, stride=run * span_y), :] = value
            else:
                out_ref[0, y, pl.ds(row, 8, stride=run), :] = value


def kinetics(place, supersat, toeplitz, column, parts, early, groups, batches):
    span_x, span_y, span_z = supersat.shape
    bin_count = toeplitz.shape[0]
    native = span_y % 8 == 0
    if native:
        out_shape = (bin_count, span_x, span_y, span_z)
        out_spec = pl.BlockSpec((bin_count, 1, span_y, span_z), lambda i: (0, i, 0, 0))
    else:
        out_shape = (span_x, span_y, bin_count, span_z)
        out_spec = layer_spec(out_shape)
    out, depletion = pl.pallas_call(
        functools.partial(kinetics_kernel, batches, groups, native),
        grid=(span_x,),
        in_specs=[smem_spec(), layer_spec(supersat.shape)]
        + [vmem_spec()] * 2
        + [layer_spec(array.shape) for array in parts + early],
        out_specs=[out_spec, layer_spec(supersat.shape)],
        out_shape=[
            jax.ShapeDtypeStruct(out_shape, jnp.float32),
            jax.ShapeDtypeStruct(supersat.shape, jnp.float32),
        ],
        scratch_shapes=[pltpu.VMEM((bin_count * span_y, span_z), jnp.float32)],
        compiler_params=params(),
        cost_estimate=cost(0, 50_000_000),
        name="kinetics",
    )(place, supersat, toeplitz, column, *parts, *early)
    return (out if native else jnp.transpose(out, (2, 0, 1, 3)), depletion)


def assemble_kernel(batches, place_ref, *refs):
    *parts, out_ref = refs
    for back in range(batches):
        source = lax.bitwise_xor(place_ref[0], back)
        for layer in range(out_ref.shape[0]):
            out_ref[layer, source] = parts[back][layer]


def assembled(place, parts, batches):
    span_x, span_y, span_z = parts[0].shape
    out = pl.pallas_call(
        functools.partial(assemble_kernel, batches),
        in_specs=[pl.BlockSpec(memory_space=pltpu.SMEM)] + [vmem_spec()] * batches,
        out_specs=vmem_spec(),
        out_shape=jax.ShapeDtypeStruct((span_x, batches, span_y, span_z), jnp.float32),
        compiler_params=params(),
        name="assemble",
    )(place, *parts)
    return out.reshape(span_x, batches * span_y, span_z)


def swapped(array, axis, partner):
    count = lax.axis_size(axis)
    pairs = [(i, partner(i)) for i in range(count) if 0 <= partner(i) < count]
    return lax.ppermute(array, axis, pairs)


def with_partner(array):
    return swapped(array, "space", lambda i: i ^ 1)


def with_other(array):
    return swapped(array, "space", lambda i: ((i + 1) ^ 1) - 1)


def body(population, velocity, supersat, kernel):
    batches = lax.axis_size("bins")
    place = jnp.stack([lax.axis_index("bins"), lax.axis_index("space")]).astype(jnp.int32)
    toeplitz, column = tables(kernel)
    codes, *slabs = coded_slab(population, velocity)
    groups = len(slabs)
    inside = with_partner(codes)
    outside = [with_other(slab) for slab in slabs]
    coefs = weights(place, velocity, inside, outside[0])
    parts = [[] for _ in range(batches)]
    moved = []
    for group in range(groups):
        after = list(moved[:1]) + ([row[group - 2] for row in parts[1:]] if group > 1 else [])
        moved = transported(
            place, population, inside, outside[group], coefs, group, batches, after
        )
        for ahead, array in enumerate(moved):
            if ahead:
                array = swapped(array, "bins", lambda i: i ^ ahead)
            parts[ahead].append(array)
    early = []
    if groups > 1:
        flat = [part for row in parts for part in row[:-1]]
        early = [unpacked(place, flat, groups, batches)]
    last = [row[-1] for row in parts]
    out, own = kinetics(place, supersat, toeplitz, column, last, early, groups, batches)
    others = [own] + [swapped(own, "bins", lambda i: i ^ ahead) for ahead in range(1, batches)]
    return (out, assembled(place, others, batches))


def solution(mesh):
    in_specs = (
        P("bins", "space", None, None),
        P(None, "space", None, None),
        P("space", "bins", None),
        P(),
    )
    out_specs = (P(None, "space", "bins", None), P("space", None, None))
    return jax.shard_map(body, mesh=mesh, in_specs=in_specs, out_specs=out_specs, check_vma=False)
```

```python
import functools

import jax
import jax.numpy as jnp
from jax import lax
from jax.experimental import pallas as pl
from jax.experimental.pallas import tpu as pltpu
from jax.sharding import PartitionSpec as P

STEPS = 3
KSTEPS = 8

COURANT = 0.3
GROW = 0.4
BETA = 0.5

POWER = 9
SCALE = 256.0
GROUP = 16
VMEM_LIMIT = 32 * 1024 * 1024
CODE_LIMIT = 56 * 1024 * 1024


def encode(scaled):
    square = scaled * scaled
    fourth = square * square
    return (fourth * fourth * scaled).astype(jnp.bfloat16)


def decode(code):
    wide = code.astype(jnp.float32)
    size = jnp.exp(jnp.log(jnp.abs(wide)) * (1.0 / POWER))
    return jnp.where(wide < 0.0, -size, size)


def params(limit=VMEM_LIMIT):
    return pltpu.CompilerParams(vmem_limit_bytes=limit)


def cost(flops, size):
    return pl.CostEstimate(flops=flops, bytes_accessed=size, transcendentals=0)


def vmem_spec():
    return pl.BlockSpec(memory_space=pltpu.VMEM)


def smem_spec():
    return pl.BlockSpec(memory_space=pltpu.SMEM)


def code_kernel(pop_any, velocity_any, all_ref, *rest):
    *group_refs, pop_ref, velocity_ref, sems = rest
    bins, span_x = pop_ref.shape[:2]
    copies = [
        pltpu.make_async_copy(
            pop_any.at[pl.ds(number * GROUP, GROUP)],
            pop_ref.at[pl.ds(number * GROUP, GROUP)],
            sems.at[number],
        )
        for number in range(len(group_refs))
    ]
    copies.append(pltpu.make_async_copy(velocity_any, velocity_ref, sems.at[len(group_refs)]))
    for copy in copies:
        copy.start()
    all_ref[pl.ds(bins + 3, GROUP - 3)] = jnp.zeros(
        (GROUP - 3,) + all_ref.shape[1:], jnp.bfloat16
    )
    for number, group_ref in enumerate(group_refs):
        copies[number].wait()

        def layer(x, carry, number=number, group_ref=group_ref):
            for index in range(0, GROUP, 4):
                code = encode(pop_ref[pl.ds(number * GROUP + index, 4), x] * SCALE)
                all_ref[pl.ds(number * GROUP + index, 4), x] = code
                group_ref[pl.ds(index, 4), x] = code
            return carry

        lax.fori_loop(0, span_x, layer, 0)
    copies[-1].wait()
    group_refs[0][pl.ds(GROUP, 3)] = velocity_ref[...]
    all_ref[pl.ds(bins, 3)] = velocity_ref[...]


def coded_slab(population, velocity):
    bins = population.shape[0]
    span = population.shape[1:]
    groups = bins // GROUP
    sizes = [bins + GROUP, GROUP + 3] + [GROUP] * (groups - 1)
    return pl.pallas_call(
        code_kernel,
        in_specs=[pl.BlockSpec(memory_space=pltpu.HBM)] * 2,
        out_specs=[vmem_spec()] * len(sizes),
        out_shape=[jax.ShapeDtypeStruct((size,) + span, jnp.bfloat16) for size in sizes],
        scratch_shapes=[
            pltpu.VMEM(population.shape, jnp.float32),
            pltpu.VMEM(velocity.shape, jnp.bfloat16),
            pltpu.SemaphoreType.DMA((groups + 1,)),
        ],
        compiler_params=params(CODE_LIMIT),
        cost_estimate=cost(0, 6_000_000),
        name="code_slab",
    )(population, velocity)


def weight_kernel(place_ref, own_ref, inside_ref, outside_ref, coef_ref, vel_ref):
    _, span_x, span_y, span_z = own_ref.shape
    odd = lax.rem(place_ref[1], 2)
    inside = 2 * span_x * (1 - odd)
    for axis in range(3):
        for x in range(span_x):
            vel_ref[axis, inside + x] = inside_ref[axis, x].astype(jnp.float32)
            vel_ref[axis, span_x + x] = own_ref[axis, x].astype(jnp.float32)
            vel_ref[axis, 2 * span_x - inside + x] = outside_ref[GROUP + axis, x].astype(jnp.float32)
    rows = lax.broadcasted_iota(jnp.int32, (span_y, span_z), 0)
    lanes = lax.broadcasted_iota(jnp.int32, (span_y, span_z), 1)

    def layer(x, carry):
        kept_in = jnp.where((x + 1 >= span_x) | (place_ref[1] > 0), 1.0, 0.0)
        scale = COURANT * kept_in
        rise = lambda value: jnp.maximum(value, 0.0) * scale
        fall = lambda value: jnp.minimum(value, 0.0) * (-scale)
        vel_x, next_x = vel_ref[0, x + 1], vel_ref[0, x + 2]
        vel_y, vel_z = vel_ref[1, x + 1], vel_ref[2, x + 1]
        next_y = jnp.where(rows < span_y - 1, pltpu.roll(vel_y, span_y - 1, 0), 0.0)
        next_z = jnp.where(lanes < span_z - 1, pltpu.roll(vel_z, span_z - 1, 1), 0.0)
        coef_ref[0, x] = kept_in - (
            rise(next_x) + fall(vel_x) + rise(next_y) + fall(vel_y) + rise(next_z) + fall(vel_z)
        )
        coef_ref[1, x] = rise(vel_x)
        coef_ref[2, x] = fall(next_x)
        coef_ref[3, x] = rise(vel_y)
        coef_ref[4, x] = fall(next_y)
        coef_ref[5, x] = jnp.where(lanes > 0, rise(vel_z), 0.0)
        coef_ref[6, x] = fall(next_z)
        return carry

    lax.fori_loop(0, coef_ref.shape[1], layer, 0)


def weights(place, velocity, inside, outside):
    span = velocity.shape[1:]
    whole = lambda shape: pl.BlockSpec(shape, lambda i: (0, 0, 0, 0))
    tail = inside.shape[0] // GROUP - 1
    return pl.pallas_call(
        weight_kernel,
        grid=(1,),
        in_specs=[
            smem_spec(),
            whole(velocity.shape),
            pl.BlockSpec((GROUP,) + span, lambda i: (tail, 0, 0, 0)),
            whole(outside.shape),
        ],
        out_specs=whole((7, 3 * span[0] - 2) + span[1:]),
        out_shape=jax.ShapeDtypeStruct((7, 3 * span[0] - 2) + span[1:], jnp.float32),
        scratch_shapes=[pltpu.VMEM((3, 3 * span[0]) + span[1:], jnp.float32)],
        compiler_params=params(),
        cost_estimate=cost(0, 4_000_000),
        name="weights",
    )(place, velocity, inside, outside)


RIM = 8
PIECE = 32


def transport_kernel(batches, place_ref, pop_ref, inside_ref, outside_ref, coef_ref, *rest):
    *outs, first, second, third, last = rest[-batches - 4 :]
    _, span_x, span_y, span_z = pop_ref.shape
    bins = GROUP
    zeros = jnp.zeros((bins, RIM, span_z), jnp.float32)
    for ref in (first, second, third):
        for x in range(ref.shape[0]):
            ref[x, :, pl.ds(0, RIM)] = zeros
            ref[x, :, pl.ds(RIM + span_y, RIM)] = zeros
    inside = 2 * span_x * (1 - lax.rem(place_ref[1], 2))
    body = pl.ds(RIM, span_y)

    def fill(x, carry):
        for index in range(bins):
            first[inside + x, index, body] = decode(inside_ref[index, x])
            first[span_x + x, index, body] = pop_ref[index, x] * SCALE
            first[2 * span_x - inside + x, index, body] = decode(outside_ref[index, x])
        return carry

    lax.fori_loop(0, span_x, fill, 0)

    for src, dst, shift, rim in (
        (first, second, 0, RIM),
        (second, third, 1, RIM),
        (third, last, 2, 0),
    ):

        def layer(x, carry, src=src, dst=dst, shift=shift, rim=rim):
            for y in range(0, span_y, 8):
                here, down, up = (pl.ds(RIM + y + by, 8) for by in (0, -1, 1))
                weight = [coef_ref[k, x + shift, pl.ds(y, 8)] for k in range(7)]
                for index in range(bins):
                    centre = src[x + 1, index, here]
                    total = weight[0] * centre
                    total += weight[1] * src[x, index, here]
                    total += weight[2] * src[x + 2, index, here]
                    total += weight[3] * src[x + 1, index, down]
                    total += weight[4] * src[x + 1, index, up]
                    total += weight[5] * pltpu.roll(centre, 1, 1)
                    total += weight[6] * pltpu.roll(centre, span_z - 1, 1)
                    dst[x, index, pl.ds(rim + y, 8)] = total
            return carry

        lax.fori_loop(0, dst.shape[0], layer, 0)
    span_out = span_y // batches
    rows = last.reshape(span_x * bins * span_y, span_z)
    for ahead in range(batches):
        begin = lax.bitwise_xor(place_ref[0], ahead) * span_out
        for x in range(span_x):
            for y in range(span_out):
                at = x * bins * span_y + begin + y
                outs[ahead][x, y] = encode(rows[pl.ds(at, bins, stride=span_y), :])


def transported(place, population, inside, outside, coefs, group, batches, after):
    _, span_x, span_y, span_z = population.shape
    out = (span_x, span_y // batches, GROUP, span_z)
    block = (GROUP, span_x, span_y, span_z)
    at = lambda shape, start: pl.BlockSpec(shape, lambda i: (start, 0, 0, 0))
    return pl.pallas_call(
        functools.partial(transport_kernel, batches),
        grid=(1,),
        in_specs=[smem_spec(), at(block, group), at(block, group), at(block, 0), at(coefs.shape, 0)]
        + [pl.BlockSpec(memory_space=pl.ANY)] * len(after),
        out_specs=[at(out, 0)] * batches,
        out_shape=[jax.ShapeDtypeStruct(out, jnp.bfloat16)] * batches,
        scratch_shapes=[
            pltpu.VMEM((depth, GROUP, span_y + 2 * RIM, span_z), jnp.float32)
            for depth in (3 * span_x, 3 * span_x - 2, 3 * span_x - 4)
        ]
        + [pltpu.VMEM((span_x, GROUP, span_y, span_z), jnp.float32)],
        compiler_params=params(),
        cost_estimate=cost(0, 18_000_000),
        name="transport",
    )(place, population, inside, outside, coefs, *after)


def bins_of_rows(shape, dim):
    count = shape[dim]
    row = lax.broadcasted_iota(jnp.int32, shape, dim)
    return (row % 8) * (count // 8) + row // 8


def table_kernel(kernel_ref, toeplitz_ref, column_ref):
    bin_count = toeplitz_ref.shape[0]
    square = (bin_count, bin_count)
    wide = jnp.broadcast_to(kernel_ref[...], (bin_count, 2 * bin_count))
    turned = pltpu.roll(wide, 0, 1, stride=1, stride_axis=0)[:, :bin_count]
    column = jnp.broadcast_to(jnp.sum(turned, axis=1, keepdims=True), column_ref.shape)
    plain = turned.T.astype(jnp.bfloat16)
    other = lax.broadcasted_iota(jnp.int32, square, 1)
    moves = jnp.where(bins_of_rows(square, 0) == other, 1.0, 0.0)
    exact = functools.partial(
        jnp.dot, preferred_element_type=jnp.float32, precision=lax.Precision.HIGHEST
    )
    column_ref[...] = exact(moves, column) + GROW / BETA
    moves = moves.astype(jnp.bfloat16)
    half = jnp.dot(moves, plain, preferred_element_type=jnp.float32).astype(jnp.bfloat16)
    toeplitz_ref[...] = jnp.dot(half, moves.T, preferred_element_type=jnp.float32).astype(
        jnp.bfloat16
    )


def tables(kernel):
    bin_count = kernel.shape[0]
    return pl.pallas_call(
        table_kernel,
        in_specs=[vmem_spec()],
        out_specs=[vmem_spec()] * 2,
        out_shape=[
            jax.ShapeDtypeStruct((bin_count, bin_count), jnp.bfloat16),
            jax.ShapeDtypeStruct((bin_count, 128), jnp.float32),
        ],
        compiler_params=params(),
        name="tables",
    )(jnp.concatenate([kernel, jnp.zeros_like(kernel)])[None, :])


def unpack(place_ref, parts, first, groups, batches, bin_count, store):
    run = bin_count // 8
    count = len(parts) // batches
    for back in range(batches):
        source = lax.bitwise_xor(place_ref[0], back) * (groups * GROUP)
        for index in range(count):
            part = parts[back * count + index]
            begin = source + (first + index) * GROUP
            at = lax.rem(begin, run) * 8 + begin // run
            for y in range(part.shape[1]):
                value = decode(part[0, y]) * (1.0 / SCALE)
                store(pl.ds(y * bin_count + at, GROUP, stride=8), value)


def unpack_kernel(batches, groups, place_ref, *refs):
    *parts, out_ref = refs
    _, rows, span_z = out_ref.shape
    layer = out_ref.reshape(rows, span_z)

    def store(where, value):
        layer[where, :] = value

    unpack(place_ref, parts, 0, groups, batches, groups * GROUP * batches, store)


def layer_spec(shape):
    return pl.BlockSpec((1,) + shape[1:], lambda i: (i,) + (0,) * (len(shape) - 1))


def unpacked(place, parts, groups, batches):
    span_x, span_y, _, span_z = parts[0].shape
    shape = (span_x, span_y * groups * GROUP * batches, span_z)
    return pl.pallas_call(
        functools.partial(unpack_kernel, batches, groups),
        grid=(span_x,),
        in_specs=[smem_spec()] + [layer_spec(part.shape) for part in parts],
        out_specs=layer_spec(shape),
        out_shape=jax.ShapeDtypeStruct(shape, jnp.float32),
        compiler_params=params(),
        cost_estimate=cost(0, 12_000_000),
        name="unpack",
    )(place, *parts)


def kinetics_kernel(batches, groups, native, place_ref, supersat_ref, toeplitz_ref, column_ref, *rest):
    *parts, out_ref, depletion_ref, state = rest
    bin_count = toeplitz_ref.shape[0]
    span_y, span_z = supersat_ref.shape[1:]
    run = bin_count // 8
    tiles = bin_count // span_z
    count = span_y // tiles
    if groups > 1:
        *parts, early_ref = parts
        state[...] = early_ref[0]

    def store(where, value):
        state[where, :] = value

    unpack(place_ref, parts, groups - 1, groups, batches, bin_count, store)
    ratio = (bins_of_rows((bin_count, span_z), 0).astype(jnp.float32) + 1.0) / bin_count
    masses = ratio * ratio * ratio

    def mass(y):
        return jnp.sum(
            masses * state[pl.ds(y * bin_count, bin_count), :], axis=0, keepdims=True
        )

    for y in range(span_y):
        depletion_ref[0, pl.ds(y, 1), :] = mass(y)

    def steps(*sums):
        eighth = lax.broadcasted_iota(jnp.int32, (8, span_z), 0)
        pieces = bin_count // PIECE

        def multiply(number, rounded):
            stage = number // 2 % 2
            pltpu.matmul_push_rhs(rounded, stage, number % 2)
            for piece in range(pieces):
                pltpu.matmul_acc_lhs(
                    sums[number * pieces + piece],
                    toeplitz_ref[pl.ds(piece * PIECE, PIECE), :],
                    load_staged_rhs=None if piece else stage,
                )

        def advance(number):
            speeds, lowers = [], []
            for tile in range(tiles):
                y = number * tiles + tile
                row = supersat_ref[0, pl.ds(y, 1), :]
                speeds.append(BETA * jnp.broadcast_to(row, (8, span_z)))
                last = state[pl.ds((y + 1) * bin_count - 8, 8), :]
                lowers.append(jnp.where(eighth > 0, pltpu.roll(last, 1, 0), 0.0))
            rounded = []
            for row in range(0, bin_count, 16):
                if row % PIECE == 0:
                    product = pltpu.matmul_pop(sums[number * pieces + row // PIECE])
                pairs = [[] for _ in range(tiles)]
                for at in (row, row + 8):
                    column = column_ref[pl.ds(at, 8), :]
                    for tile in range(tiles):
                        where = pl.ds((number * tiles + tile) * bin_count + at, 8)
                        now = state[where, :]
                        change = (GROW / BETA) * lowers[tile] - column * now
                        change += product[
                            at % PIECE : at % PIECE + 8, tile * span_z : (tile + 1) * span_z
                        ]
                        new = now + speeds[tile] * change
                        state[where, :] = new
                        pairs[tile].append(new)
                        lowers[tile] = now
                rounded.append(
                    jnp.concatenate(
                        [jnp.concatenate(pair, axis=0) for pair in pairs], axis=1
                    ).astype(jnp.bfloat16)
                )
            return jnp.concatenate(rounded, axis=0)

        for number in range(count):
            values = [
                state[pl.ds((number * tiles + tile) * bin_count, bin_count), :]
                for tile in range(tiles)
            ]
            multiply(number, jnp.concatenate(values, axis=1).astype(jnp.bfloat16))

        def substep(index, carry):
            for number in range(count):
                multiply(number, advance(number))
            return carry

        lax.fori_loop(0, KSTEPS - 1, substep, 0)
        for number in range(count):
            advance(number)

    pl.run_scoped(
        steps,
        *(
            pltpu.ACC(mxu_id=number % 2)((PIECE, bin_count), jnp.float32)
            for number in range(count)
            for piece in range(bin_count // PIECE)
        ),
    )
    for y in range(span_y):
        depletion_ref[0, pl.ds(y, 1), :] = mass(y) - depletion_ref[0, pl.ds(y, 1), :]
        if native:
            rows = out_ref.reshape(bin_count * span_y, span_z)
        for row in range(run):
            value = state[pl.ds(y * bin_count + 8 * row, 8), :]
            if native:
                rows[pl.ds(row * span_y + y, 8, stride=run * span_y), :] = value
            else:
                out_ref[0, y, pl.ds(row, 8, stride=run), :] = value


def kinetics(place, supersat, toeplitz, column, parts, early, groups, batches):
    span_x, span_y, span_z = supersat.shape
    bin_count = toeplitz.shape[0]
    native = span_y % 8 == 0
    if native:
        out_shape = (bin_count, span_x, span_y, span_z)
        out_spec = pl.BlockSpec((bin_count, 1, span_y, span_z), lambda i: (0, i, 0, 0))
    else:
        out_shape = (span_x, span_y, bin_count, span_z)
        out_spec = layer_spec(out_shape)
    out, depletion = pl.pallas_call(
        functools.partial(kinetics_kernel, batches, groups, native),
        grid=(span_x,),
        in_specs=[smem_spec(), layer_spec(supersat.shape)]
        + [vmem_spec()] * 2
        + [layer_spec(array.shape) for array in parts + early],
        out_specs=[out_spec, layer_spec(supersat.shape)],
        out_shape=[
            jax.ShapeDtypeStruct(out_shape, jnp.float32),
            jax.ShapeDtypeStruct(supersat.shape, jnp.float32),
        ],
        scratch_shapes=[pltpu.VMEM((bin_count * span_y, span_z), jnp.float32)],
        compiler_params=params(),
        cost_estimate=cost(0, 50_000_000),
        name="kinetics",
    )(place, supersat, toeplitz, column, *parts, *early)
    return (out if native else jnp.transpose(out, (2, 0, 1, 3)), depletion)


def assemble_kernel(batches, place_ref, *refs):
    *parts, out_ref = refs
    for back in range(batches):
        source = lax.bitwise_xor(place_ref[0], back)
        for layer in range(out_ref.shape[0]):
            out_ref[layer, source] = parts[back][layer]


def assembled(place, parts, batches):
    span_x, span_y, span_z = parts[0].shape
    out = pl.pallas_call(
        functools.partial(assemble_kernel, batches),
        in_specs=[pl.BlockSpec(memory_space=pltpu.SMEM)] + [vmem_spec()] * batches,
        out_specs=vmem_spec(),
        out_shape=jax.ShapeDtypeStruct((span_x, batches, span_y, span_z), jnp.float32),
        compiler_params=params(),
        name="assemble",
    )(place, *parts)
    return out.reshape(span_x, batches * span_y, span_z)


def swapped(array, axis, partner):
    count = lax.axis_size(axis)
    pairs = [(i, partner(i)) for i in range(count) if 0 <= partner(i) < count]
    return lax.ppermute(array, axis, pairs)


def with_partner(array):
    return swapped(array, "space", lambda i: i ^ 1)


def with_other(array):
    return swapped(array, "space", lambda i: ((i + 1) ^ 1) - 1)


def body(population, velocity, supersat, kernel):
    batches = lax.axis_size("bins")
    place = jnp.stack([lax.axis_index("bins"), lax.axis_index("space")]).astype(jnp.int32)
    toeplitz, column = tables(kernel)
    codes, *slabs = coded_slab(population, velocity)
    groups = len(slabs)
    inside = with_partner(codes)
    outside = [with_other(slab) for slab in slabs]
    coefs = weights(place, velocity, inside, outside[0])
    parts = [[] for _ in range(batches)]
    moved = []
    for group in range(groups):
        after = list(moved[:1]) + ([row[group - 2] for row in parts[1:]] if group > 1 else [])
        moved = transported(
            place, population, inside, outside[group], coefs, group, batches, after
        )
        for ahead, array in enumerate(moved):
            if ahead:
                array = swapped(array, "bins", lambda i: i ^ ahead)
            parts[ahead].append(array)
    early = []
    if groups > 1:
        flat = [part for row in parts for part in row[:-1]]
        early = [unpacked(place, flat, groups, batches)]
    last = [row[-1] for row in parts]
    out, own = kinetics(place, supersat, toeplitz, column, last, early, groups, batches)
    others = [own] + [swapped(own, "bins", lambda i: i ^ ahead) for ahead in range(1, batches)]
    return (out, assembled(place, others, batches))


def solution(mesh):
    in_specs = (
        P("bins", "space", None, None),
        P(None, "space", None, None),
        P("space", "bins", None),
        P(),
    )
    out_specs = (P(None, "space", "bins", None), P("space", None, None))
    return jax.shard_map(body, mesh=mesh, in_specs=in_specs, out_specs=out_specs, check_vma=False)
```

```python
import functools

import jax
import jax.numpy as jnp
from jax import lax
from jax.experimental import pallas as pl
from jax.experimental.pallas import tpu as pltpu
from jax.sharding import PartitionSpec as P

STEPS = 3
KSTEPS = 8

COURANT = 0.3
GROW = 0.4
BETA = 0.5

POWER = 9
SCALE = 256.0
GROUP = 16
VMEM_LIMIT = 32 * 1024 * 1024
CODE_LIMIT = 56 * 1024 * 1024


def encode(scaled):
    square = scaled * scaled
    fourth = square * square
    return (fourth * fourth * scaled).astype(jnp.bfloat16)


def decode(code):
    wide = code.astype(jnp.float32)
    size = jnp.exp(jnp.log(jnp.abs(wide)) * (1.0 / POWER))
    return jnp.where(wide < 0.0, -size, size)


def params(limit=VMEM_LIMIT):
    return pltpu.CompilerParams(vmem_limit_bytes=limit)


def cost(flops, size):
    return pl.CostEstimate(flops=flops, bytes_accessed=size, transcendentals=0)


def vmem_spec():
    return pl.BlockSpec(memory_space=pltpu.VMEM)


def smem_spec():
    return pl.BlockSpec(memory_space=pltpu.SMEM)


def code_kernel(pop_any, velocity_any, all_ref, *rest):
    *group_refs, pop_ref, velocity_ref, sems = rest
    bins, span_x = pop_ref.shape[:2]
    copies = [
        pltpu.make_async_copy(
            pop_any.at[pl.ds(number * GROUP, GROUP)],
            pop_ref.at[pl.ds(number * GROUP, GROUP)],
            sems.at[number],
        )
        for number in range(len(group_refs))
    ]
    copies.append(pltpu.make_async_copy(velocity_any, velocity_ref, sems.at[len(group_refs)]))
    for copy in copies:
        copy.start()
    all_ref[pl.ds(bins + 3, GROUP - 3)] = jnp.zeros(
        (GROUP - 3,) + all_ref.shape[1:], jnp.bfloat16
    )
    for number, group_ref in enumerate(group_refs):
        copies[number].wait()

        def layer(x, carry, number=number, group_ref=group_ref):
            for index in range(0, GROUP, 4):
                code = encode(pop_ref[pl.ds(number * GROUP + index, 4), x] * SCALE)
                all_ref[pl.ds(number * GROUP + index, 4), x] = code
                group_ref[pl.ds(index, 4), x] = code
            return carry

        lax.fori_loop(0, span_x, layer, 0)
    copies[-1].wait()
    group_refs[0][pl.ds(GROUP, 3)] = velocity_ref[...]
    all_ref[pl.ds(bins, 3)] = velocity_ref[...]


def coded_slab(population, velocity):
    bins = population.shape[0]
    span = population.shape[1:]
    groups = bins // GROUP
    sizes = [bins + GROUP, GROUP + 3] + [GROUP] * (groups - 1)
    return pl.pallas_call(
        code_kernel,
        in_specs=[pl.BlockSpec(memory_space=pltpu.HBM)] * 2,
        out_specs=[vmem_spec()] * len(sizes),
        out_shape=[jax.ShapeDtypeStruct((size,) + span, jnp.bfloat16) for size in sizes],
        scratch_shapes=[
            pltpu.VMEM(population.shape, jnp.float32),
            pltpu.VMEM(velocity.shape, jnp.bfloat16),
            pltpu.SemaphoreType.DMA((groups + 1,)),
        ],
        compiler_params=params(CODE_LIMIT),
        cost_estimate=cost(0, 6_000_000),
        name="code_slab",
    )(population, velocity)


def weight_kernel(place_ref, own_ref, inside_ref, outside_ref, coef_ref, vel_ref):
    _, span_x, span_y, span_z = own_ref.shape
    odd = lax.rem(place_ref[1], 2)
    inside = 2 * span_x * (1 - odd)
    for axis in range(3):
        for x in range(span_x):
            vel_ref[axis, inside + x] = inside_ref[axis, x].astype(jnp.float32)
            vel_ref[axis, span_x + x] = own_ref[axis, x].astype(jnp.float32)
            vel_ref[axis, 2 * span_x - inside + x] = outside_ref[GROUP + axis, x].astype(jnp.float32)
    rows = lax.broadcasted_iota(jnp.int32, (span_y, span_z), 0)
    lanes = lax.broadcasted_iota(jnp.int32, (span_y, span_z), 1)

    def layer(x, carry):
        kept_in = jnp.where((x + 1 >= span_x) | (place_ref[1] > 0), 1.0, 0.0)
        scale = COURANT * kept_in
        rise = lambda value: jnp.maximum(value, 0.0) * scale
        fall = lambda value: jnp.minimum(value, 0.0) * (-scale)
        vel_x, next_x = vel_ref[0, x + 1], vel_ref[0, x + 2]
        vel_y, vel_z = vel_ref[1, x + 1], vel_ref[2, x + 1]
        next_y = jnp.where(rows < span_y - 1, pltpu.roll(vel_y, span_y - 1, 0), 0.0)
        next_z = jnp.where(lanes < span_z - 1, pltpu.roll(vel_z, span_z - 1, 1), 0.0)
        coef_ref[0, x] = kept_in - (
            rise(next_x) + fall(vel_x) + rise(next_y) + fall(vel_y) + rise(next_z) + fall(vel_z)
        )
        coef_ref[1, x] = rise(vel_x)
        coef_ref[2, x] = fall(next_x)
        coef_ref[3, x] = rise(vel_y)
        coef_ref[4, x] = fall(next_y)
        coef_ref[5, x] = jnp.where(lanes > 0, rise(vel_z), 0.0)
        coef_ref[6, x] = fall(next_z)
        return carry

    lax.fori_loop(0, coef_ref.shape[1], layer, 0)


def weights(place, velocity, inside, outside):
    span = velocity.shape[1:]
    whole = lambda shape: pl.BlockSpec(shape, lambda i: (0, 0, 0, 0))
    tail = inside.shape[0] // GROUP - 1
    return pl.pallas_call(
        weight_kernel,
        grid=(1,),
        in_specs=[
            smem_spec(),
            whole(velocity.shape),
            pl.BlockSpec((GROUP,) + span, lambda i: (tail, 0, 0, 0)),
            whole(outside.shape),
        ],
        out_specs=whole((7, 3 * span[0] - 2) + span[1:]),
        out_shape=jax.ShapeDtypeStruct((7, 3 * span[0] - 2) + span[1:], jnp.float32),
        scratch_shapes=[pltpu.VMEM((3, 3 * span[0]) + span[1:], jnp.float32)],
        compiler_params=params(),
        cost_estimate=cost(0, 4_000_000),
        name="weights",
    )(place, velocity, inside, outside)


RIM = 8
PIECE = 32


def transport_kernel(batches, place_ref, pop_ref, inside_ref, outside_ref, coef_ref, *rest):
    *outs, first, second, third, last = rest[-batches - 4 :]
    _, span_x, span_y, span_z = pop_ref.shape
    bins = GROUP
    zeros = jnp.zeros((bins, RIM, span_z), jnp.float32)
    for ref in (first, second, third):
        for x in range(ref.shape[0]):
            ref[x, :, pl.ds(0, RIM)] = zeros
            ref[x, :, pl.ds(RIM + span_y, RIM)] = zeros
    inside = 2 * span_x * (1 - lax.rem(place_ref[1], 2))
    body = pl.ds(RIM, span_y)

    def fill(x, carry):
        for index in range(bins):
            first[inside + x, index, body] = decode(inside_ref[index, x])
            first[span_x + x, index, body] = pop_ref[index, x] * SCALE
            first[2 * span_x - inside + x, index, body] = decode(outside_ref[index, x])
        return carry

    lax.fori_loop(0, span_x, fill, 0)

    for src, dst, shift, rim in (
        (first, second, 0, RIM),
        (second, third, 1, RIM),
        (third, last, 2, 0),
    ):

        def layer(x, carry, src=src, dst=dst, shift=shift, rim=rim):
            for y in range(0, span_y, 8):
                here, down, up = (pl.ds(RIM + y + by, 8) for by in (0, -1, 1))
                weight = [coef_ref[k, x + shift, pl.ds(y, 8)] for k in range(7)]
                for index in range(bins):
                    centre = src[x + 1, index, here]
                    total = weight[0] * centre
                    total += weight[1] * src[x, index, here]
                    total += weight[2] * src[x + 2, index, here]
                    total += weight[3] * src[x + 1, index, down]
                    total += weight[4] * src[x + 1, index, up]
                    total += weight[5] * pltpu.roll(centre, 1, 1)
                    total += weight[6] * pltpu.roll(centre, span_z - 1, 1)
                    dst[x, index, pl.ds(rim + y, 8)] = total
            return carry

        lax.fori_loop(0, dst.shape[0], layer, 0)
    span_out = span_y // batches
    rows = last.reshape(span_x * bins * span_y, span_z)
    for ahead in range(batches):
        begin = lax.bitwise_xor(place_ref[0], ahead) * span_out
        for x in range(span_x):
            if span_out == 8:
                begin = pl.multiple_of(begin, 8)
                turned = jnp.swapaxes(last[x, :, pl.ds(begin, span_out)], 0, 1)
                for y in range(span_out):
                    outs[ahead][x, y] = encode(turned[y])
                continue
            for y in range(span_out):
                at = x * bins * span_y + begin + y
                outs[ahead][x, y] = encode(rows[pl.ds(at, bins, stride=span_y), :])


def transported(place, population, inside, outside, coefs, group, batches, after):
    _, span_x, span_y, span_z = population.shape
    out = (span_x, span_y // batches, GROUP, span_z)
    block = (GROUP, span_x, span_y, span_z)
    at = lambda shape, start: pl.BlockSpec(shape, lambda i: (start, 0, 0, 0))
    return pl.pallas_call(
        functools.partial(transport_kernel, batches),
        grid=(1,),
        in_specs=[smem_spec(), at(block, group), at(block, group), at(block, 0), at(coefs.shape, 0)]
        + [pl.BlockSpec(memory_space=pl.ANY)] * len(after),
        out_specs=[at(out, 0)] * batches,
        out_shape=[jax.ShapeDtypeStruct(out, jnp.bfloat16)] * batches,
        scratch_shapes=[
            pltpu.VMEM((depth, GROUP, span_y + 2 * RIM, span_z), jnp.float32)
            for depth in (3 * span_x, 3 * span_x - 2, 3 * span_x - 4)
        ]
        + [pltpu.VMEM((span_x, GROUP, span_y, span_z), jnp.float32)],
        compiler_params=params(),
        cost_estimate=cost(0, 18_000_000),
        name="transport",
    )(place, population, inside, outside, coefs, *after)


def bins_of_rows(shape, dim):
    count = shape[dim]
    row = lax.broadcasted_iota(jnp.int32, shape, dim)
    return (row % 8) * (count // 8) + row // 8


def table_kernel(kernel_ref, toeplitz_ref, column_ref):
    bin_count = toeplitz_ref.shape[0]
    square = (bin_count, bin_count)
    wide = jnp.broadcast_to(kernel_ref[...], (bin_count, 2 * bin_count))
    turned = pltpu.roll(wide, 0, 1, stride=1, stride_axis=0)[:, :bin_count]
    column = jnp.broadcast_to(jnp.sum(turned, axis=1, keepdims=True), column_ref.shape)
    plain = turned.T.astype(jnp.bfloat16)
    other = lax.broadcasted_iota(jnp.int32, square, 1)
    moves = jnp.where(bins_of_rows(square, 0) == other, 1.0, 0.0)
    exact = functools.partial(
        jnp.dot, preferred_element_type=jnp.float32, precision=lax.Precision.HIGHEST
    )
    column_ref[...] = exact(moves, column) + GROW / BETA
    moves = moves.astype(jnp.bfloat16)
    half = jnp.dot(moves, plain, preferred_element_type=jnp.float32).astype(jnp.bfloat16)
    toeplitz_ref[...] = jnp.dot(half, moves.T, preferred_element_type=jnp.float32).astype(
        jnp.bfloat16
    )


def tables(kernel):
    bin_count = kernel.shape[0]
    return pl.pallas_call(
        table_kernel,
        in_specs=[vmem_spec()],
        out_specs=[vmem_spec()] * 2,
        out_shape=[
            jax.ShapeDtypeStruct((bin_count, bin_count), jnp.bfloat16),
            jax.ShapeDtypeStruct((bin_count, 128), jnp.float32),
        ],
        compiler_params=params(),
        name="tables",
    )(jnp.concatenate([kernel, jnp.zeros_like(kernel)])[None, :])


def unpack(place_ref, parts, first, groups, batches, bin_count, store):
    run = bin_count // 8
    count = len(parts) // batches
    for back in range(batches):
        source = lax.bitwise_xor(place_ref[0], back) * (groups * GROUP)
        for index in range(count):
            part = parts[back * count + index]
            begin = source + (first + index) * GROUP
            at = lax.rem(begin, run) * 8 + begin // run
            for y in range(part.shape[1]):
                value = decode(part[0, y]) * (1.0 / SCALE)
                store(pl.ds(y * bin_count + at, GROUP, stride=8), value)


def unpack_kernel(batches, groups, place_ref, *refs):
    *parts, out_ref = refs
    _, rows, span_z = out_ref.shape
    layer = out_ref.reshape(rows, span_z)

    def store(where, value):
        layer[where, :] = value

    unpack(place_ref, parts, 0, groups, batches, groups * GROUP * batches, store)


def layer_spec(shape):
    return pl.BlockSpec((1,) + shape[1:], lambda i: (i,) + (0,) * (len(shape) - 1))


def unpacked(place, parts, groups, batches):
    span_x, span_y, _, span_z = parts[0].shape
    shape = (span_x, span_y * groups * GROUP * batches, span_z)
    return pl.pallas_call(
        functools.partial(unpack_kernel, batches, groups),
        grid=(span_x,),
        in_specs=[smem_spec()] + [layer_spec(part.shape) for part in parts],
        out_specs=layer_spec(shape),
        out_shape=jax.ShapeDtypeStruct(shape, jnp.float32),
        compiler_params=params(),
        cost_estimate=cost(0, 12_000_000),
        name="unpack",
    )(place, *parts)


def kinetics_kernel(batches, groups, native, place_ref, supersat_ref, toeplitz_ref, column_ref, *rest):
    *parts, out_ref, depletion_ref, state = rest
    bin_count = toeplitz_ref.shape[0]
    span_y, span_z = supersat_ref.shape[1:]
    run = bin_count // 8
    tiles = bin_count // span_z
    count = span_y // tiles
    if groups > 1:
        *parts, early_ref = parts
        state[...] = early_ref[0]

    def store(where, value):
        state[where, :] = value

    unpack(place_ref, parts, groups - 1, groups, batches, bin_count, store)
    ratio = (bins_of_rows((bin_count, span_z), 0).astype(jnp.float32) + 1.0) / bin_count
    masses = ratio * ratio * ratio

    def mass(y):
        return jnp.sum(
            masses * state[pl.ds(y * bin_count, bin_count), :], axis=0, keepdims=True
        )

    for y in range(span_y):
        depletion_ref[0, pl.ds(y, 1), :] = mass(y)

    def steps(*sums):
        eighth = lax.broadcasted_iota(jnp.int32, (8, span_z), 0)
        pieces = bin_count // PIECE

        def multiply(number, rounded):
            stage = number // 2 % 2
            pltpu.matmul_push_rhs(rounded, stage, number % 2)
            for piece in range(pieces):
                pltpu.matmul_acc_lhs(
                    sums[number * pieces + piece],
                    toeplitz_ref[pl.ds(piece * PIECE, PIECE), :],
                    load_staged_rhs=None if piece else stage,
                )

        def advance(number):
            speeds, lowers = [], []
            for tile in range(tiles):
                y = number * tiles + tile
                row = supersat_ref[0, pl.ds(y, 1), :]
                speeds.append(BETA * jnp.broadcast_to(row, (8, span_z)))
                last = state[pl.ds((y + 1) * bin_count - 8, 8), :]
                lowers.append(jnp.where(eighth > 0, pltpu.roll(last, 1, 0), 0.0))
            rounded = []
            for row in range(0, bin_count, 16):
                if row % PIECE == 0:
                    product = pltpu.matmul_pop(sums[number * pieces + row // PIECE])
                pairs = [[] for _ in range(tiles)]
                for at in (row, row + 8):
                    column = column_ref[pl.ds(at, 8), :]
                    for tile in range(tiles):
                        where = pl.ds((number * tiles + tile) * bin_count + at, 8)
                        now = state[where, :]
                        change = (GROW / BETA) * lowers[tile] - column * now
                        change += product[
                            at % PIECE : at % PIECE + 8, tile * span_z : (tile + 1) * span_z
                        ]
                        new = now + speeds[tile] * change
                        state[where, :] = new
                        pairs[tile].append(new)
                        lowers[tile] = now
                rounded.append(
                    jnp.concatenate(
                        [jnp.concatenate(pair, axis=0) for pair in pairs], axis=1
                    ).astype(jnp.bfloat16)
                )
            return jnp.concatenate(rounded, axis=0)

        for number in range(count):
            values = [
                state[pl.ds((number * tiles + tile) * bin_count, bin_count), :]
                for tile in range(tiles)
            ]
            multiply(number, jnp.concatenate(values, axis=1).astype(jnp.bfloat16))

        def substep(index, carry):
            for number in range(count):
                multiply(number, advance(number))
            return carry

        lax.fori_loop(0, KSTEPS - 1, substep, 0)
        for number in range(count):
            advance(number)

    pl.run_scoped(
        steps,
        *(
            pltpu.ACC(mxu_id=number % 2)((PIECE, bin_count), jnp.float32)
            for number in range(count)
            for piece in range(bin_count // PIECE)
        ),
    )
    for y in range(span_y):
        depletion_ref[0, pl.ds(y, 1), :] = mass(y) - depletion_ref[0, pl.ds(y, 1), :]
    for row in range(run):
        values = [state[pl.ds(y * bin_count + 8 * row, 8), :] for y in range(span_y)]
        if native:
            turned = jnp.swapaxes(jnp.stack(values), 0, 1)
            for index in range(8):
                out_ref[index * run + row, 0] = turned[index]
        else:
            for y, value in enumerate(values):
                out_ref[0, y, pl.ds(row, 8, stride=run), :] = value


def kinetics(place, supersat, toeplitz, column, parts, early, groups, batches):
    span_x, span_y, span_z = supersat.shape
    bin_count = toeplitz.shape[0]
    native = span_y % 8 == 0
    if native:
        out_shape = (bin_count, span_x, span_y, span_z)
        out_spec = pl.BlockSpec((bin_count, 1, span_y, span_z), lambda i: (0, i, 0, 0))
    else:
        out_shape = (span_x, span_y, bin_count, span_z)
        out_spec = layer_spec(out_shape)
    out, depletion = pl.pallas_call(
        functools.partial(kinetics_kernel, batches, groups, native),
        grid=(span_x,),
        in_specs=[smem_spec(), layer_spec(supersat.shape)]
        + [vmem_spec()] * 2
        + [layer_spec(array.shape) for array in parts + early],
        out_specs=[out_spec, layer_spec(supersat.shape)],
        out_shape=[
            jax.ShapeDtypeStruct(out_shape, jnp.float32),
            jax.ShapeDtypeStruct(supersat.shape, jnp.float32),
        ],
        scratch_shapes=[pltpu.VMEM((bin_count * span_y, span_z), jnp.float32)],
        compiler_params=params(),
        cost_estimate=cost(0, 50_000_000),
        name="kinetics",
    )(place, supersat, toeplitz, column, *parts, *early)
    return (out if native else jnp.transpose(out, (2, 0, 1, 3)), depletion)


def assemble_kernel(batches, place_ref, *refs):
    *parts, out_ref = refs
    for back in range(batches):
        source = lax.bitwise_xor(place_ref[0], back)
        for layer in range(out_ref.shape[0]):
            out_ref[layer, source] = parts[back][layer]


def assembled(place, parts, batches):
    span_x, span_y, span_z = parts[0].shape
    out = pl.pallas_call(
        functools.partial(assemble_kernel, batches),
        in_specs=[pl.BlockSpec(memory_space=pltpu.SMEM)] + [vmem_spec()] * batches,
        out_specs=vmem_spec(),
        out_shape=jax.ShapeDtypeStruct((span_x, batches, span_y, span_z), jnp.float32),
        compiler_params=params(),
        name="assemble",
    )(place, *parts)
    return out.reshape(span_x, batches * span_y, span_z)


def swapped(array, axis, partner):
    count = lax.axis_size(axis)
    pairs = [(i, partner(i)) for i in range(count) if 0 <= partner(i) < count]
    return lax.ppermute(array, axis, pairs)


def with_partner(array):
    return swapped(array, "space", lambda i: i ^ 1)


def with_other(array):
    return swapped(array, "space", lambda i: ((i + 1) ^ 1) - 1)


def body(population, velocity, supersat, kernel):
    batches = lax.axis_size("bins")
    place = jnp.stack([lax.axis_index("bins"), lax.axis_index("space")]).astype(jnp.int32)
    toeplitz, column = tables(kernel)
    codes, *slabs = coded_slab(population, velocity)
    groups = len(slabs)
    inside = with_partner(codes)
    outside = [with_other(slab) for slab in slabs]
    coefs = weights(place, velocity, inside, outside[0])
    parts = [[] for _ in range(batches)]
    moved = []
    for group in range(groups):
        after = list(moved[:1]) + ([row[group - 2] for row in parts[1:]] if group > 1 else [])
        moved = transported(
            place, population, inside, outside[group], coefs, group, batches, after
        )
        for ahead, array in enumerate(moved):
            if ahead:
                array = swapped(array, "bins", lambda i: i ^ ahead)
            parts[ahead].append(array)
    early = []
    if groups > 1:
        flat = [part for row in parts for part in row[:-1]]
        early = [unpacked(place, flat, groups, batches)]
    last = [row[-1] for row in parts]
    out, own = kinetics(place, supersat, toeplitz, column, last, early, groups, batches)
    others = [own] + [swapped(own, "bins", lambda i: i ^ ahead) for ahead in range(1, batches)]
    return (out, assembled(place, others, batches))


def solution(mesh):
    in_specs = (
        P("bins", "space", None, None),
        P(None, "space", None, None),
        P("space", "bins", None),
        P(),
    )
    out_specs = (P(None, "space", "bins", None), P("space", None, None))
    return jax.shard_map(body, mesh=mesh, in_specs=in_specs, out_specs=out_specs, check_vma=False)
```
